128 devices in a mesh: seq: 64 (over x_lo, z, y, core), head: 2 (over x_hi).
Axes of the slice: x: 4 (x_hi: 2, x_lo: 2; x = x_hi * 2 + x_lo), y: 4, z: 4, core: 2. Of those that a mesh axis runs over, the one named last changes fastest.
Arguments:
- video_query: bfloat16 [131072, 2048], P('seq', 'head'), may hold values from -360 to 360
- video_kv: bfloat16 [2, 131072, 2048], P(None, 'seq', 'head'), may hold values from -360 to 360
- video_clip: int32 [131072], P('seq'), may hold values from 0 to 7, never falling along the last dimension, each value on 1 to 98304 neighbouring positions
- audio_hidden: bfloat16 [256, 2048], replicated, may hold values from -6 to 6
- audio_qkv_weight: bfloat16 [64, 128, 1536], P('seq', None, 'head'), may hold values from -0.125 to 0.125
- audio_clip: int32 [256], replicated, may hold values from 0 to 7, never falling along the last dimension, each value on 1 to 192 neighbouring positions
- audio_out_weight: bfloat16 [2048, 2048], P('head', 'seq'), may hold values from -0.125 to 0.125
Outputs:
- video_attn: bfloat16 [131072, 2048], P('seq', 'head')
- audio_out: bfloat16 [256, 2048], P('head', 'seq')
The draws below stay inside these ranges and needn't reach their ends.
Inputs may be any that keep to these rules, and one draw needn't show every extreme that they name: `video_clip`: rows of one clip are consecutive; every clip number appears among the video rows. `audio_clip`: rows of one clip are consecutive; every clip number appears among the audio rows.
All inputs are finite; a program needn't handle non-finite values.
Results may differ from the reference program's by a relative error of at most 0.009.
The reference program's roundings to bfloat16 on the way count: a program that leaves them out, or rounds other values in their place, can miss the bound.
Values may be sent and summed in bfloat16 or wider, within the bound.
A program may use at most 128 MiB of HBM per device.

```python
import math
import jax
import jax.numpy as jnp
import numpy as np
from jax import lax

H = 32
HD = 64
DA = 2048
NA = 256
VTOK_DEV = 2048
CLIPS = 8
NV = 131072
N_SEQ = 64
N_HEAD = 2


def scaled_rows(key, shape):
    key_base = jax.random.fold_in(key, 0)
    base = jnp.clip(jax.random.normal(key_base, shape, jnp.float32), -6.0, 6.0)
    return base


def draw_video_query(key, part):
    values = scaled_rows(jax.random.fold_in(key, 11), (NV, H * HD))
    return values.astype(jnp.bfloat16)


def draw_video_kv(key, part):
    keys = scaled_rows(jax.random.fold_in(key, 23), (NV, H * HD))
    noise = jnp.clip(jax.random.normal(jax.random.fold_in(key, 29), (NV // VTOK_DEV, VTOK_DEV, H * HD), jnp.float32), -6.0, 6.0)
    offsets = 3.0 * jnp.clip(jax.random.normal(jax.random.fold_in(key, 31), (NV // VTOK_DEV, 1, H * HD), jnp.float32), -5.0, 5.0)
    values = (noise + offsets).reshape(NV, H * HD)
    return jnp.stack([keys, values]).astype(jnp.bfloat16)


def level_of(rng, dims, pieces, low, largest):
    def one(dim, shards_of):
        steps = jax.random.uniform(jax.random.fold_in(jax.random.fold_in(rng, 6), dim), (shards_of,), jnp.float32, low / len(pieces), largest / len(pieces))
        return jnp.repeat(jnp.exp(steps), dims[dim] // shards_of).reshape((-1,) + (1,) * (len(dims) - dim - 1))

    loudness = one(*pieces[0])
    for cut in pieces[1:]:
        loudness = loudness * one(*cut)
    return loudness


def length_profile(number_of, total, bound, skew):
    portions = [(1 << 20) // math.isqrt(grade ** skew) + 1 for grade in range(2, number_of + 1)]
    surplus, counts = total - bound - (number_of - 1), [1] * (number_of - 1)
    while surplus > 0:
        free = [i for i in range(number_of - 1) if counts[i] < bound]
        pool, budget = sum([portions[i] for i in free]), surplus
        for i in free:
            addition = min(bound - counts[i], max(1, budget * portions[i] // pool), surplus)
            counts[i] = counts[i] + addition
            surplus = surplus - addition
    return np.array([bound] + counts)


def ragged_sizes(rng, number_of, total, reach, slope):
    if number_of == 2:
        one = jax.random.randint(rng, (), max(1, total - reach), min(reach, total - 1) + 1)
        return jnp.stack([one, total - one])
    tallies = jnp.asarray(length_profile(number_of, total, reach, slope), jnp.int32)
    pairs = (number_of - 1) // 2
    giver, taker = tallies[1:1 + 2 * pairs:2], tallies[2:2 + 2 * pairs:2]
    margin = jnp.minimum(giver - 1, reach - taker)
    moved = jax.random.randint(jax.random.fold_in(rng, 1), (pairs,), 0, 1 << 20) % (margin + 1)
    tallies = tallies.at[1:1 + 2 * pairs:2].set(giver - moved).at[2:2 + 2 * pairs:2].set(taker + moved)
    return tallies[jax.random.permutation(jax.random.fold_in(rng, 2), number_of)]


def scatter_about(rng, dims, deviation, most, shards=(), held_as=jnp.bfloat16):
    values = jax.random.normal(rng, dims, jnp.float32) * deviation
    if len(shards) > 0:
        values = level_of(rng, dims, shards, -0.22, 0.18) * values
    return jnp.clip(values, min=-most, max=most).astype(held_as)


def setup_inputs(seed: int = 0) -> dict:
    streams_of = jax.random.split(jax.random.key(seed), 8)
    video_query = draw_video_query(jax.random.fold_in(streams_of[7], 71), 0)
    video_kv = draw_video_kv(jax.random.fold_in(streams_of[7], 71), 0)
    video_clip = jnp.searchsorted(jnp.cumsum(ragged_sizes(streams_of[2], CLIPS, NV, NV * 3 // 4, 2)), jnp.arange(NV), side="right").astype(jnp.int32)
    audio_hidden = scatter_about(streams_of[3], (NA, DA), 1.0, 6.0)
    audio_qkv_weight = scatter_about(streams_of[4], (N_SEQ, DA // 16, 3 * H * HD * 16 // N_SEQ), DA ** -0.5, 0.125, ((0, 64), (2, 2)))
    audio_clip = jnp.searchsorted(jnp.cumsum(ragged_sizes(streams_of[5], CLIPS, NA, NA * 3 // 4, 2)), jnp.arange(NA), side="right").astype(jnp.int32)
    audio_out_weight = scatter_about(streams_of[6], (H * HD, DA), (H * HD) ** -0.5, 0.125, ((0, 2), (1, 64)))
    return dict(video_query=video_query, video_kv=video_kv, video_clip=video_clip, audio_hidden=audio_hidden, audio_qkv_weight=audio_qkv_weight, audio_clip=audio_clip, audio_out_weight=audio_out_weight)


NEG = -1e30


def video_head(inputs, same):
    query, key, value = inputs
    scores = jnp.dot(query, key.T, preferred_element_type=jnp.float32) * 0.125
    scores = jnp.where(same, scores, NEG)
    top = jnp.max(scores, axis=1, keepdims=True)
    expo = jnp.exp(scores - top)
    probs = (expo / jnp.sum(expo, axis=1, keepdims=True)).astype(jnp.bfloat16)
    return jnp.dot(probs, value, preferred_element_type=jnp.float32)


def audio_head(inputs, same_t):
    query, key, value = inputs
    scores = jnp.dot(query, key.T, preferred_element_type=jnp.float32) * 0.125
    scores = jnp.where(same_t, scores, NEG)
    top = jnp.max(scores, axis=1, keepdims=True)
    weights = jnp.where(same_t, jnp.exp(scores - top), jnp.float32(0.0))
    denominator = jnp.sum(weights, axis=1, keepdims=True)
    numerator = jnp.dot(weights.astype(jnp.bfloat16), value, preferred_element_type=jnp.float32)
    return numerator / denominator


def reference(video_query, video_kv, video_clip, audio_hidden, audio_qkv_weight, audio_clip, audio_out_weight):
    quarters = N_SEQ // 16
    group_heads = H // N_HEAD
    columns = 3 * group_heads * HD // quarters
    laid = audio_qkv_weight.reshape(quarters, 16, DA // 16, N_HEAD, columns)
    laid = jnp.transpose(laid, (1, 2, 3, 0, 4)).reshape(DA, N_HEAD, 3, group_heads, HD)
    flat_weight = jnp.transpose(laid, (0, 2, 1, 3, 4)).reshape(DA, 3 * H * HD)
    audio_qkv = jnp.dot(audio_hidden, flat_weight, preferred_element_type=jnp.float32).astype(jnp.bfloat16)
    audio_qkv = audio_qkv.reshape(NA, 3, H, HD)
    audio_q = jnp.transpose(audio_qkv[:, 0], (1, 0, 2))
    audio_k = jnp.transpose(audio_qkv[:, 1], (1, 0, 2))
    audio_v = jnp.transpose(audio_qkv[:, 2], (1, 0, 2))
    vid_q = jnp.transpose(video_query.reshape(NV, H, HD), (1, 0, 2))
    vid_k = jnp.transpose(video_kv[0].reshape(NV, H, HD), (1, 0, 2))
    vid_v = jnp.transpose(video_kv[1].reshape(NV, H, HD), (1, 0, 2))
    same = video_clip[:, None] == audio_clip[None, :]
    same_t = audio_clip[:, None] == video_clip[None, :]
    video_out = lax.map(lambda item: video_head(item, same), (vid_q, audio_k, audio_v))
    video_attn = jnp.transpose(video_out, (1, 0, 2)).reshape(NV, H * HD).astype(jnp.bfloat16)
    audio_res = lax.map(lambda item: audio_head(item, same_t), (audio_q, vid_k, vid_v))
    audio_attn = jnp.transpose(audio_res, (1, 0, 2)).reshape(NA, H * HD).astype(jnp.bfloat16)
    audio_out = jnp.dot(audio_attn, audio_out_weight, preferred_element_type=jnp.float32).astype(jnp.bfloat16)
    return video_attn, audio_out
```

```python
import functools

import jax
import jax.numpy as jnp
from jax import lax
from jax.experimental import pallas as pl
from jax.experimental.pallas import tpu as pltpu
from jax.sharding import PartitionSpec as P

F32 = jnp.float32
BF = jnp.bfloat16
NT = (((1,), (1,)), ((), ()))
BIG = -1e30
MESH = pl.DeviceIdType.MESH
VMEM = pl.BlockSpec(memory_space=pltpu.VMEM)
ANY = pl.BlockSpec(memory_space=pl.ANY)
CHIPS = 32
GROUP = 8


def place():
    seq = lax.axis_index("seq")
    head = lax.axis_index("head")
    return seq // 2, seq % 2, head


def remote(src, dst, send, recv, chip, core, head):
    return pltpu.make_async_remote_copy(
        src_ref=src,
        dst_ref=dst,
        send_sem=send,
        recv_sem=recv,
        device_id=(chip * 2 + core, head),
        device_id_type=MESH,
    )


def greet(chip, core, head, with_head):
    barrier = pltpu.get_barrier_semaphore()

    def one(i, _):
        to = lax.rem(chip + i, CHIPS)
        pl.semaphore_signal(barrier, inc=1, device_id=(to * 2 + core, head), device_id_type=MESH)
        return 0

    lax.fori_loop(1, CHIPS, one, 0)
    pl.semaphore_signal(
        barrier, inc=1, device_id=(chip * 2 + 1 - core, head), device_id_type=MESH
    )
    count = CHIPS
    if with_head:
        pl.semaphore_signal(
            barrier, inc=1, device_id=(chip * 2 + core, 1 - head), device_id_type=MESH
        )
        count += 1
    pl.semaphore_wait(barrier, count)


def spread(groups, send_sem, recv_sem, pass_send, pass_recv, chip, core, head, slot):
    own = slot(chip, core)

    def send(i):
        to = lax.rem(chip + i, CHIPS)
        return remote(own, own, send_sem.at[i], recv_sem.at[i], to, core, head)

    def start(i, _):
        send(i).start()
        return 0

    def hand_on(i):
        frm = lax.rem(chip + CHIPS - i, CHIPS)
        block = slot(frm, core)
        return remote(block, block, pass_send.at[i], pass_recv.at[i], chip, 1 - core, head)

    def handed(i):
        frm = lax.rem(chip + CHIPS - i, CHIPS)
        block = slot(frm, 1 - core)
        return remote(block, block, pass_send.at[i], pass_recv.at[i], chip, 1 - core, head)

    def begin():
        hand_on(0).start()
        lax.fori_loop(1, CHIPS, start, 0)

    def relay(i, _):
        frm = lax.rem(chip + CHIPS - i, CHIPS)
        block = slot(frm, core)
        remote(block, block, send_sem.at[i], recv_sem.at[i], frm, core, head).wait_recv()
        hand_on(i).start()
        return 0

    def middle():
        lax.fori_loop(1, CHIPS, relay, 0)

    def finish():
        def arrived(i, _):
            handed(i).wait_recv()
            hand_on(i).wait_send()
            return 0

        def sent(i, _):
            send(i).wait_send()
            return 0

        lax.fori_loop(0, CHIPS, arrived, 0)
        lax.fori_loop(1, CHIPS, sent, 0)

    return begin, middle, finish


def project_kernel(x, w, out, xs, part, near, total, far, sem, s2, r2, s3, r3, s4, r4):
    chip, core, head = place()
    quarter, g = chip // GROUP, chip % GROUP
    fg = g * 2 + core
    load = pltpu.make_async_copy(
        x.at[:, pl.ds(pl.multiple_of(fg * 128, 128), 128)], xs, sem.at[0]
    )
    load.start()
    load.wait()
    part[...] = jnp.dot(xs[...], w[0], preferred_element_type=F32)
    greet(chip, core, head, False)
    theirs = part.at[pl.ds(pl.multiple_of((1 - core) * 128, 128), 128)]
    swap = remote(theirs, near, sem.at[1], sem.at[2], chip, 1 - core, head)
    swap.start()
    swap.wait_recv()
    total[...] = part[pl.ds(pl.multiple_of(core * 128, 128), 128), :] + near[...]

    def scatter(i):
        to = lax.rem(g + i, GROUP)
        rows = total.at[pl.ds(pl.multiple_of(to * 16, 16), 16)]
        return remote(rows, far.at[i], s2.at[i], r2.at[i], quarter * GROUP + to, core, head)

    for i in range(1, GROUP):
        scatter(i).start()
    acc = total[pl.ds(pl.multiple_of(g * 16, 16), 16), :]
    for i in range(1, GROUP):
        scatter(i).wait_recv()
        acc = acc + far[i]

    def slot(c, k):
        row = pl.multiple_of((k * GROUP + lax.rem(c, GROUP)) * 16, 16)
        return out.at[c // GROUP, pl.ds(row, 16)]

    slot(chip, core)[...] = acc.astype(BF)
    begin, middle, finish = spread(None, s3, r3, s4, r4, chip, core, head, slot)
    begin()
    middle()
    finish()
    for i in range(1, GROUP):
        scatter(i).wait_send()
    swap.wait_send()


def project(x, w):
    return pl.pallas_call(
        project_kernel,
        out_shape=jax.ShapeDtypeStruct((4, 256, 768), BF),
        in_specs=[ANY, VMEM],
        out_specs=VMEM,
        scratch_shapes=[
            pltpu.VMEM((256, 128), BF),
            pltpu.VMEM((256, 768), F32),
            pltpu.VMEM((128, 768), F32),
            pltpu.VMEM((128, 768), F32),
            pltpu.VMEM((GROUP, 16, 768), F32),
            pltpu.SemaphoreType.DMA((3,)),
            pltpu.SemaphoreType.DMA((GROUP,)),
            pltpu.SemaphoreType.DMA((GROUP,)),
            pltpu.SemaphoreType.DMA((CHIPS,)),
            pltpu.SemaphoreType.DMA((CHIPS,)),
            pltpu.SemaphoreType.DMA((CHIPS,)),
            pltpu.SemaphoreType.DMA((CHIPS,)),
        ],
        compiler_params=pltpu.CompilerParams(
            collective_id=0, has_side_effects=True, vmem_limit_bytes=16 * 2**20
        ),
    )(x, w)


def lanes(j):
    return pl.ds(pl.multiple_of(j * 128, 128), 128)


def columns(qkv, block):
    return qkv[block // 6, :, lanes(block % 6)]


def both_heads(x, mask):
    lane = lax.broadcasted_iota(jnp.int32, x.shape, 1)
    zero = jnp.zeros_like(x)
    x = (x.astype(F32) * 0.125).astype(BF)
    first = jnp.concatenate([jnp.where(lane < 64, x, zero), mask], 1)
    second = jnp.concatenate([jnp.where(lane >= 64, x, zero), mask], 1)
    return jnp.concatenate([first, second], 0)


def audio_kernel(qkv, mask, hot, kv, numer, stat, sa, sb, ma, mb):
    size = 512
    pieces = kv.shape[1] // size
    stat[...] = jnp.zeros_like(stat)
    lane = lax.broadcasted_iota(jnp.int32, (256, 128), 1)
    ones = jnp.ones((size, 128), BF)

    def query(j):
        return both_heads(columns(qkv, j), mask[...])

    def score(j, q2, c, s_ref, top):
        rows = pl.ds(c * size, size)
        keys = jnp.concatenate([kv[0, rows, lanes(j)], hot[rows, :]], 1)
        s = lax.dot_general(q2, keys, NT, preferred_element_type=F32)
        s_ref[:, c * size : (c + 1) * size] = s
        for t in range(size // 128):
            piece = s[:, t * 128 : (t + 1) * 128]
            top = piece if top is None else jnp.maximum(top, piece)
        return top

    def keep(top, m_ref):
        m_ref[...] = jnp.broadcast_to(jnp.max(top, axis=1, keepdims=True), (512, 128))

    def weigh(j, top, c, s_ref, acc):
        rows = pl.ds(c * size, size)
        wide = jnp.concatenate([top] * (size // 128), 1)
        weights = jnp.exp(s_ref[:, c * size : (c + 1) * size] - wide).astype(BF)
        values = jnp.concatenate([kv[1, rows, lanes(j)], ones], 1)
        r = jnp.dot(weights, values, preferred_element_type=F32)
        return r if acc is None else acc + r

    def step(j, following, s_ref, m_ref, s_next, m_next):
        q2 = query(following)
        top, acc, now = None, None, m_ref[...]
        for c in range(pieces):
            top = score(following, q2, c, s_next, top)
            acc = weigh(j, now, c, s_ref, acc)
        keep(top, m_next)
        numer[:, lanes(j)] = jnp.where(lane < 64, acc[:256, :128], acc[256:, :128])
        st = stat[...]
        st = jnp.where(lane == 2 * j, now[:256], st)
        st = jnp.where(lane == 2 * j + 1, now[256:], st)
        st = jnp.where(lane == 2 * j + 64, acc[:256, 128:], st)
        st = jnp.where(lane == 2 * j + 65, acc[256:, 128:], st)
        stat[...] = st

    q2, top = query(0), None
    for c in range(pieces):
        top = score(0, q2, c, sa, top)
    keep(top, ma)

    def two(i, _):
        step(2 * i, 2 * i + 1, sa, ma, sb, mb)
        step(2 * i + 1, jnp.minimum(2 * i + 2, 7), sb, mb, sa, ma)
        return 0

    lax.fori_loop(0, 4, two, 0)


def audio_part(qkv, mask, hot, kv):
    return pl.pallas_call(
        audio_kernel,
        out_shape=(
            jax.ShapeDtypeStruct((256, 1024), F32),
            jax.ShapeDtypeStruct((256, 128), F32),
        ),
        in_specs=[VMEM] * 4,
        out_specs=(VMEM, VMEM),
        scratch_shapes=[
            pltpu.VMEM((512, 2048), F32),
            pltpu.VMEM((512, 2048), F32),
            pltpu.VMEM((512, 128), F32),
            pltpu.VMEM((512, 128), F32),
        ],
        compiler_params=pltpu.CompilerParams(vmem_limit_bytes=40 * 2**20),
    )(qkv, mask, hot, kv)


def video_pair(j, qkv, mask, hot, vq, vout):
    size = 1024
    lane = lax.broadcasted_iota(jnp.int32, (size, 128), 1)
    k2 = both_heads(columns(qkv, j + 8), mask[...])
    values = jnp.concatenate([columns(qkv, j + 16), jnp.ones((256, 128), BF)], 1)
    for c in range(vq.shape[0] // size):
        rows = pl.ds(c * size, size)
        q = jnp.concatenate([vq[rows, lanes(j)], hot[rows, :]], 1)
        s = lax.dot_general(q, k2, NT, preferred_element_type=F32)
        r = []
        for h in range(2):
            sh = s[:, h * 256 : (h + 1) * 256]
            p = jnp.exp(sh - jnp.max(sh, axis=1, keepdims=True)).astype(BF)
            r.append(jnp.dot(p, values, preferred_element_type=F32))
        num = jnp.where(lane < 64, r[0][:, :128], r[1][:, :128])
        den = jnp.where(lane < 64, r[0][:, 128:], r[1][:, 128:])
        vout[rows, lanes(j)] = (num / den).astype(BF)


def video_kernel(qkv, mask, hot, vq, vout):
    def one(j, _):
        video_pair(j, qkv, mask, hot, vq, vout)
        return 0

    lax.fori_loop(0, 8, one, 0)


def video_part(qkv, mask, hot, vq):
    return pl.pallas_call(
        video_kernel,
        out_shape=jax.ShapeDtypeStruct(vq.shape, BF),
        in_specs=[VMEM] * 4,
        out_specs=VMEM,
        compiler_params=pltpu.CompilerParams(vmem_limit_bytes=40 * 2**20),
    )(qkv, mask, hot, vq)


def widened(f, first):
    n = f.shape[0]
    lane = lax.broadcasted_iota(jnp.int32, (n, 128), 1)
    out = []
    for p in range(4):
        a = jnp.broadcast_to(f[:, first + 2 * p : first + 2 * p + 1], (n, 128))
        b = jnp.broadcast_to(f[:, first + 2 * p + 1 : first + 2 * p + 2], (n, 128))
        out.append(jnp.where(lane < 64, a, b))
    return jnp.concatenate(out, 1)


def of_core(f, core, shift):
    return jnp.where(core == 0, f[:, shift : shift + 8], f[:, shift + 8 : shift + 16])


def finish_kernel(
    with_video, numer, stat, wout, qkv, mask, hot, vq, *refs
):
    if with_video:
        vout, refs = refs[0], refs[1:]
    out, rn, rs, comb, land, gath, mine, back, swap, sem, s2, r2, s3, r3, s4, r4 = refs
    chip, core, head = place()

    def video(j0, j1):
        if with_video:
            def one(j, _):
                video_pair(j, qkv, mask, hot, vq, vout)
                return 0

            lax.fori_loop(j0, j1, one, 0)

    greet(chip, core, head, True)
    send_n = remote(
        numer.at[:, pl.ds(pl.multiple_of((1 - core) * 512, 512), 512)],
        rn, sem.at[0], sem.at[1], chip, 1 - core, head,
    )
    send_s = remote(stat, rs, sem.at[2], sem.at[3], chip, 1 - core, head)
    send_n.start()
    send_s.start()
    video(0, 1)
    send_s.wait_recv()
    send_n.wait_recv()

    lane = lax.broadcasted_iota(jnp.int32, (256, 128), 1)
    a, b = stat[...], rs[...]
    top = jnp.maximum(a, b)
    fa = jnp.where(lane < 64, jnp.exp(a - top), 0.0)
    fb = jnp.where(lane < 64, jnp.exp(b - top), 0.0)
    den = a * pltpu.roll(fa, 64, 1) + b * pltpu.roll(fb, 64, 1)
    comb[:, 512:] = jnp.where(lane < 64, top, den)
    own = numer[:, pl.ds(pl.multiple_of(core * 512, 512), 512)]
    wa, wb = widened(of_core(fa, core, 0), 0), widened(of_core(fb, core, 0), 0)
    comb[:, :512] = own * wa + rn[...] * wb

    def scatter(i):
        to = lax.rem(chip + i, CHIPS)
        rows = comb.at[pl.ds(pl.multiple_of(to * 8, 8), 8)]
        return remote(rows, land.at[i], s2.at[i], r2.at[i], to, core, head)

    def start(i, _):
        scatter(i).start()
        return 0

    lax.fori_loop(1, CHIPS, start, 0)
    land[0] = comb[pl.ds(pl.multiple_of(chip * 8, 8), 8), :]
    video(1, 4)

    def landed(i, _):
        scatter(i).wait_recv()
        return 0

    lax.fori_loop(1, CHIPS, landed, 0)
    stats = [land[i, :, 512:] for i in range(CHIPS)]
    top = functools.reduce(jnp.maximum, stats)
    lane = lax.broadcasted_iota(jnp.int32, (8, 128), 1)
    total = jnp.zeros((8, 512), F32)
    den = jnp.zeros((8, 128), F32)
    for i in range(CHIPS):
        f = jnp.where(lane < 64, jnp.exp(stats[i] - top), 0.0)
        den = den + stats[i] * pltpu.roll(f, 64, 1)
        total = total + land[i, :, :512] * widened(of_core(f, core, 0), 0)
    attn = total / widened(of_core(den, core, 64), 0)

    def slot(c, k):
        return gath.at[k, c]

    slot(chip, core)[...] = jnp.concatenate([attn[:, :256], attn[:, 256:]], 0).astype(BF)
    begin, middle, end = spread(None, s3, r3, s4, r4, chip, core, head, slot)
    begin()
    video(4, 6)
    middle()
    video(6, 7)
    end()
    acc = None
    for k in range(2):
        rows = gath[k].reshape(CHIPS * 16, 256)
        for h in range(2):
            at = k * 512 + h * 256
            r = jnp.dot(rows, wout[at : at + 256, :], preferred_element_type=F32)
            r = r.reshape(CHIPS, 16, 32)[:, h * 8 : (h + 1) * 8]
            acc = r if acc is None else acc + r
    mine[...] = acc.reshape(256, 32)

    def folded(x):
        return jnp.concatenate([x[32 * t : 32 * t + 32] for t in range(4)], 1)

    swap[...] = folded(mine[pl.ds(pl.multiple_of((1 - head) * 128, 128), 128), :])
    across = remote(swap, back, sem.at[4], sem.at[5], chip, core, 1 - head)
    across.start()
    video(7, 8)
    across.wait_recv()
    half = folded(mine[pl.ds(pl.multiple_of(head * 128, 128), 128), :]) + back[...]
    for t in range(4):
        out[32 * t : 32 * t + 32, :] = half[:, 32 * t : 32 * t + 32].astype(BF)
    across.wait_send()
    send_n.wait_send()
    send_s.wait_send()

    def sent(i, _):
        scatter(i).wait_send()
        return 0

    lax.fori_loop(1, CHIPS, sent, 0)


def finish_part(numer, stat, wout, qkv, mask, hot, vq, with_video):
    shapes = [jax.ShapeDtypeStruct((128, 32), BF)]
    if with_video:
        shapes = [jax.ShapeDtypeStruct(vq.shape, BF)] + shapes
    return pl.pallas_call(
        functools.partial(finish_kernel, with_video),
        out_shape=tuple(shapes),
        in_specs=[VMEM] * 6 + [VMEM if with_video else ANY],
        out_specs=tuple([VMEM] * len(shapes)),
        scratch_shapes=[
            pltpu.VMEM((256, 512), F32),
            pltpu.VMEM((256, 128), F32),
            pltpu.VMEM((256, 640), F32),
            pltpu.VMEM((CHIPS, 8, 640), F32),
            pltpu.VMEM((2, CHIPS, 16, 256), BF),
            pltpu.VMEM((256, 32), F32),
            pltpu.VMEM((32, 128), F32),
            pltpu.VMEM((32, 128), F32),
            pltpu.SemaphoreType.DMA((6,)),
            pltpu.SemaphoreType.DMA((CHIPS,)),
            pltpu.SemaphoreType.DMA((CHIPS,)),
            pltpu.SemaphoreType.DMA((CHIPS,)),
            pltpu.SemaphoreType.DMA((CHIPS,)),
            pltpu.SemaphoreType.DMA((CHIPS,)),
            pltpu.SemaphoreType.DMA((CHIPS,)),
        ],
        compiler_params=pltpu.CompilerParams(
            collective_id=1, has_side_effects=True, vmem_limit_bytes=40 * 2**20
        ),
    )(numer, stat, wout, qkv, mask, hot, vq)


WITH_VIDEO = True


def shards(vq, kv, video_clip, x, w, audio_clip, wout):
    number = jnp.arange(128)
    hot = (video_clip[:, None] == number[None, :]).astype(BF)
    differs = (audio_clip[:, None] != number[None, :]) & (number[None, :] < 8)
    mask = jnp.where(differs, BIG, 0.0).astype(BF)
    qkv = project(x, w)
    numer, stat = audio_part(qkv, mask, hot, kv)
    if WITH_VIDEO:
        return finish_part(numer, stat, wout, qkv, mask, hot, vq, True)
    (audio_out,) = finish_part(numer, stat, wout, qkv, mask, hot, vq, False)
    return video_part(qkv, mask, hot, vq), audio_out


def solution(mesh):
    return jax.shard_map(
        shards,
        mesh=mesh,
        in_specs=(
            P("seq", "head"),
            P(None, "seq", "head"),
            P("seq"),
            P(),
            P("seq", None, "head"),
            P(),
            P("head", "seq"),
        ),
        out_specs=(P("seq", "head"), P("head", "seq")),
        check_vma=False,
    )
```

```python
import functools

import jax
import jax.numpy as jnp
from jax import lax
from jax.experimental import pallas as pl
from jax.experimental.pallas import tpu as pltpu
from jax.sharding import PartitionSpec as P

F32 = jnp.float32
BF = jnp.bfloat16
NT = (((1,), (1,)), ((), ()))
BIG = -1e30
MESH = pl.DeviceIdType.MESH
VMEM = pl.BlockSpec(memory_space=pltpu.VMEM)
ANY = pl.BlockSpec(memory_space=pl.ANY)
CHIPS = 32
GROUP = 8
QUARTERS = 4
WITHIN = 6
SIZE = 512


def lanes(j, width=128):
    return pl.ds(pl.multiple_of(j * width, width), width)


def rows_of(at, n):
    return pl.ds(pl.multiple_of(at, 16), n)


def remote(src, dst, send, recv, chip, core, head):
    return pltpu.make_async_remote_copy(
        src_ref=src,
        dst_ref=dst,
        send_sem=send,
        recv_sem=recv,
        device_id=(chip * 2 + core, head),
        device_id_type=MESH,
    )


def one_hot(clip, count):
    row = lax.broadcasted_iota(jnp.int32, (128, 128), 0)
    return [row == jnp.broadcast_to(clip[t : t + 1, :], (128, 128)) for t in range(count)]


def clip_mask(aclip):
    row = lax.broadcasted_iota(jnp.int32, (128, 128), 0)
    tiles = [jnp.where(same | (row >= 8), 0.0, BIG) for same in one_hot(aclip, 2)]
    return jnp.concatenate(tiles, 1)


def fill_hot(hot, vclip):
    for t, same in enumerate(one_hot(vclip, 16)):
        hot[t * 128 : (t + 1) * 128, :] = jnp.where(same, 1.0, 0.0).T.astype(BF)


def video_pair(kt, vt, mask_t, hot, vq, vout, at):
    size = 1024
    lane = lax.broadcasted_iota(jnp.int32, (size, 128), 1)
    row = lax.broadcasted_iota(jnp.int32, (128, 256), 0)
    scaled = (kt.astype(F32) * 0.125).astype(BF)
    zero = jnp.zeros_like(scaled)
    first = jnp.concatenate([jnp.where(row < 64, scaled, zero), mask_t], 0)
    second = jnp.concatenate([jnp.where(row >= 64, scaled, zero), mask_t], 0)
    keys = jnp.concatenate([first, second], 1)
    values = jnp.concatenate([vt, jnp.ones((128, 256), BF)], 0)
    for c in range(vq.shape[0] // size):
        rows = pl.ds(c * size, size)
        q = jnp.concatenate([vq[rows, at], hot[rows, :]], 1)
        s = jnp.dot(q, keys, preferred_element_type=F32)
        r = []
        for h in range(2):
            sh = s[:, h * 256 : (h + 1) * 256]
            p = jnp.exp(sh - jnp.max(sh, axis=1, keepdims=True)).astype(BF)
            r.append(lax.dot_general(p, values, NT, preferred_element_type=F32))
        num = jnp.where(lane < 64, r[0][:, :128], r[1][:, :128])
        den = jnp.where(lane < 64, r[0][:, 128:], r[1][:, 128:])
        vout[rows, at] = (num / den).astype(BF)


def widened(f, first, count):
    n = f.shape[0]
    lane = lax.broadcasted_iota(jnp.int32, (n, 128), 1)
    out = []
    for p in range(first, first + count, 2):
        a = jnp.broadcast_to(f[:, p : p + 1], (n, 128))
        b = jnp.broadcast_to(f[:, p + 1 : p + 2], (n, 128))
        out.append(jnp.where(lane < 64, a, b))
    return jnp.concatenate(out, 1)


def gather(part, mine, full, n, local, send_sem, recv_sem, pass_send, pass_recv, where):
    quarter, g, chip, core, head = where

    def block(q, k, i):
        return full.at[rows_of(((q * 2 + k) * GROUP + i) * n, n)]

    def group(q, k):
        return full.at[rows_of((q * 2 + k) * GROUP * n, GROUP * n)]

    own = block(quarter, core, g)

    def begin():
        pltpu.make_async_copy(mine, own, recv_sem.at[quarter]).start()

        def one(i, _):
            q = lax.rem(quarter + i // GROUP, QUARTERS)
            to = q * GROUP + lax.rem(g + i, GROUP)
            remote(mine, own, send_sem, recv_sem.at[quarter], to, core, head).start()
            return 0

        lax.fori_loop(1, CHIPS, one, 0)

    def relay(q):
        blocks = group(q, core)
        remote(blocks, blocks, send_sem, recv_sem.at[q], chip, 1 - core, head).wait_recv()
        remote(blocks, blocks, pass_send.at[q], pass_recv.at[q], chip, 1 - core, head).start()

    def passed(q):
        blocks = group(q, 1 - core)
        remote(blocks, blocks, pass_send.at[q], pass_recv.at[q], chip, 1 - core, head).wait_recv()

    def end():
        for q in range(QUARTERS):
            blocks = group(q, core)
            remote(
                blocks, blocks, pass_send.at[q], pass_recv.at[q], chip, 1 - core, head
            ).wait_send()
        sent = full.at[pl.ds(0, (CHIPS - 1) * n)]
        remote(sent, sent, send_sem, recv_sem.at[0], chip, 1 - core, head).wait_send()

    return begin, relay, passed, end


def main_kernel(
    x, w, vclip, aclip, kv, vq, wout,
    vout, tail, out,
    xs, ks, vs, qs, os, wt, wl, mine, qkv, hot, mask, mask_t,
    sa, sb, ma, mb, numer, stat, near_n, near_s, comb, land, attn, gath, part, swap, back,
    local, pair_out, one, bar1, bar2, bar3, bar4, bar5, bar6, bar7, bar8,
):
    seq, head = lax.axis_index("seq"), lax.axis_index("head")
    chip, core = seq // 2, seq % 2
    quarter, g = chip // GROUP, chip % GROUP
    where = (quarter, g, chip, core, head)

    load_x = pltpu.make_async_copy(x, xs, local.at[0])
    load_k = pltpu.make_async_copy(kv.at[0], ks, local.at[1])
    load_v = pltpu.make_async_copy(kv.at[1], vs, local.at[2])
    load_q = pltpu.make_async_copy(vq, qs, local.at[3])
    load_x.start()

    barrier = pltpu.get_barrier_semaphore()

    def greet(c, k, h):
        pl.semaphore_signal(barrier, inc=1, device_id=(c * 2 + k, h), device_id_type=MESH)

    def greet_chip(i, _):
        greet(lax.rem(chip + i, CHIPS), core, head)
        return 0

    def greet_near(i, _):
        greet(quarter * GROUP + lax.rem(g + i, GROUP), 1 - core, head)
        return 0

    lax.fori_loop(0, GROUP, greet_near, 0)
    lax.fori_loop(1, CHIPS, greet_chip, 0)
    greet(chip, core, 1 - head)
    load_k.start()
    load_v.start()
    load_q.start()
    wt[...] = w[0].astype(F32).T.astype(BF)
    pl.semaphore_wait(barrier, GROUP + CHIPS)

    feature = g * 2 + core

    def weights_to(i):
        to, k = lax.rem(g + i // 2, GROUP), lax.rem(core + i, 2)
        rows = wt.at[rows_of((k * GROUP + to) * 48, 48)]
        return remote(rows, wl.at[feature], one.at[0], one.at[1], quarter * GROUP + to, k, head)

    def weights_start(i, _):
        weights_to(i).start()
        return 0

    own_w = pltpu.make_async_copy(
        wt.at[rows_of((core * GROUP + g) * 48, 48)], wl.at[feature], one.at[1]
    )
    own_w.start()
    lax.fori_loop(1, 2 * GROUP, weights_start, 0)
    fill_hot(hot, vclip)
    flat = clip_mask(aclip)
    mask_t[...] = flat.astype(BF)
    mask[...] = flat.T.astype(BF)
    load_x.wait()
    remote(wl, wl, one.at[0], one.at[1], chip, 1 - core, head).wait_recv()
    columns = jnp.concatenate([wl[f] for f in range(2 * GROUP)], 1)
    mine[...] = lax.dot_general(columns, xs[...], NT, preferred_element_type=F32).astype(BF)

    begin, relay, passed, end_first = gather(
        None, mine, qkv, 48, None, one.at[2], bar1, bar2, bar3, where
    )

    @pl.when(quarter < 2)
    def _():
        begin()

    relay(0)
    relay(1)

    @pl.when(quarter >= 2)
    def _():
        begin()

    load_k.wait()
    load_v.wait()
    passed(0)
    passed(1)

    pieces = ks.shape[0] // SIZE
    lane = lax.broadcasted_iota(jnp.int32, (256, 128), 1)
    ones = jnp.ones((SIZE, 128), BF)
    stat[...] = jnp.zeros_like(stat)

    def pair_of(jj):
        return lax.rem(jj + 4 * (1 - core), 8)

    def query(jj):
        q = (qkv[lanes(pair_of(jj)), :].astype(F32) * 0.125).T
        zero = jnp.zeros_like(q)
        first = jnp.concatenate([jnp.where(lane < 64, q, zero).astype(BF), mask[...]], 1)
        second = jnp.concatenate([jnp.where(lane >= 64, q, zero).astype(BF), mask[...]], 1)
        return jnp.concatenate([first, second], 0)

    def score(jj, q2, c, s_ref, top):
        rows = pl.ds(c * SIZE, SIZE)
        keys = jnp.concatenate([ks[rows, lanes(pair_of(jj))], hot[rows, :]], 1)
        s = lax.dot_general(q2, keys, NT, preferred_element_type=F32)
        s_ref[:, c * SIZE : (c + 1) * SIZE] = s
        for t in range(SIZE // 128):
            piece = s[:, t * 128 : (t + 1) * 128]
            top = piece if top is None else jnp.maximum(top, piece)
        return top

    def keep(top, m_ref):
        m_ref[...] = jnp.broadcast_to(jnp.max(top, axis=1, keepdims=True), (512, 128))

    def weigh(jj, top, c, s_ref, acc):
        rows = pl.ds(c * SIZE, SIZE)
        wide = jnp.concatenate([top] * (SIZE // 128), 1)
        weights = jnp.exp(s_ref[:, c * SIZE : (c + 1) * SIZE] - wide).astype(BF)
        values = jnp.concatenate([vs[rows, lanes(pair_of(jj))], ones], 1)
        r = jnp.dot(weights, values, preferred_element_type=F32)
        return r if acc is None else acc + r

    def step(jj, half, following, s_ref, m_ref, s_next, m_next):
        q2 = query(following)
        top, acc, now = None, None, m_ref[...]
        for c in range(pieces):
            top = score(following, q2, c, s_next, top)
            acc = weigh(jj, now, c, s_ref, acc)
        keep(top, m_next)
        numer[half, :, lanes(jj - 4 * half)] = jnp.where(
            lane < 64, acc[:256, :128], acc[256:, :128]
        )
        st, at = stat[half], 2 * (jj - 4 * half)
        st = jnp.where(lane == at, now[:256], st)
        st = jnp.where(lane == at + 1, now[256:], st)
        st = jnp.where(lane == at + 64, acc[:256, 128:], st)
        stat[half] = jnp.where(lane == at + 65, acc[256:, 128:], st)

    def two(half, i, _):
        jj = 4 * half + 2 * i
        step(jj, half, jj + 1, sa, ma, sb, mb)
        step(jj + 1, half, jnp.minimum(jj + 2, 7), sb, mb, sa, ma)
        return 0

    q2, top = query(0), None
    for c in range(pieces):
        top = score(0, q2, c, sa, top)
    keep(top, ma)
    lax.fori_loop(0, 2, functools.partial(two, 0), 0)
    send_n = remote(numer.at[0], near_n, one.at[3], one.at[4], chip, 1 - core, head)
    send_s = remote(stat.at[0], near_s, one.at[5], one.at[6], chip, 1 - core, head)
    send_n.start()
    send_s.start()
    relay(2)
    relay(3)
    lax.fori_loop(0, 2, functools.partial(two, 1), 0)

    send_s.wait_recv()
    send_n.wait_recv()
    a, b = stat[1], near_s[...]
    top = jnp.maximum(a, b)
    high = top.astype(BF).astype(F32)
    top = high + (top - high).astype(BF).astype(F32)
    fa = jnp.where(lane < 64, jnp.exp(a - top), 0.0)
    fb = jnp.where(lane < 64, jnp.exp(b - top), 0.0)
    st = jnp.where(lane < 64, top, a * pltpu.roll(fa, 64, 1) + b * pltpu.roll(fb, 64, 1))
    high = st.astype(BF).astype(F32)
    both = numer[1] * widened(fa, 0, 8) + near_n[...] * widened(fb, 0, 8)

    def stacked(u, v):
        return jnp.concatenate(
            [u.reshape(CHIPS, 8, u.shape[1]), v.reshape(CHIPS, 8, v.shape[1])], 1
        ).astype(BF)

    comb[:, :, :256] = stacked(both[:, :256], both[:, 256:])
    comb[:, :, 256:] = stacked(high, st - high)

    def scatter_start(i, _):
        to = lax.rem(chip + i, CHIPS)
        remote(comb.at[to], land.at[i], one.at[7], one.at[8], to, core, head).start()
        return 0

    lax.fori_loop(1, CHIPS, scatter_start, 0)
    land[0] = comb[chip]

    load_q.wait()
    passed(2)
    passed(3)

    def video(j0, j1):
        def pair(j, _):
            video_pair(
                qkv[lanes(j + 8), :], qkv[lanes(j + 16), :], mask_t[...], hot, qs, os, lanes(j)
            )
            pltpu.make_async_copy(
                os.at[:, lanes(j)], vout.at[:, lanes(j)], pair_out.at[j]
            ).start()
            return 0

        lax.fori_loop(j0, j1, pair, 0)

    rest = 128 * (8 - WITHIN)
    tail[:rest, :] = qkv[1024 + 128 * WITHIN : 2048, :]
    tail[rest:, :] = qkv[2048 + 128 * WITHIN : 3072, :]
    video(0, 3)

    others = land.at[pl.ds(1, CHIPS - 1)]
    remote(others, others, one.at[7], one.at[8], chip, 1 - core, head).wait_recv()
    arrived = land[:, :, 256:].astype(F32)
    st = arrived[:, :8] + arrived[:, 8:]
    small = lax.broadcasted_iota(jnp.int32, (8, 128), 1)
    top = jnp.max(st, axis=0)
    total = jnp.zeros((16, 256), F32)
    den = jnp.zeros((8, 128), F32)
    for i in range(CHIPS):
        f = jnp.where(small < 64, jnp.exp(st[i] - top), 0.0)
        den = den + st[i] * pltpu.roll(f, 64, 1)
        scale = jnp.concatenate([widened(f, 0, 4), widened(f, 4, 4)], 0)
        total = total + land[i, :, :256].astype(F32) * scale
    scale = jnp.concatenate([widened(den, 64, 4), widened(den, 68, 4)], 0)
    attn[...] = (total / scale).astype(BF)

    begin, relay, passed, end_second = gather(
        None, attn, gath, 16, None, one.at[9], bar4, bar5, bar6, where
    )
    begin()
    video(3, 5)
    for q in range(QUARTERS):
        relay(q)
    video(5, 6)
    for q in range(QUARTERS):
        passed(q)
    acc = None
    for k in range(2):
        groups = [
            gath[(q * 2 + k) * GROUP * 16 : (q * 2 + k + 1) * GROUP * 16, :]
            for q in range(QUARTERS)
        ]
        rows = jnp.concatenate(groups, 0)
        for h in range(2):
            at = k * 512 + h * 256
            r = lax.dot_general(rows, wout[:, at : at + 256], NT, preferred_element_type=F32)
            r = r.reshape(CHIPS, 16, 32)[:, h * 8 : (h + 1) * 8]
            acc = r if acc is None else acc + r
    flat = acc.reshape(256, 32).T
    part[0] = flat[:, :128]
    part[1] = flat[:, 128:]
    across = remote(part.at[1 - head], back, one.at[10], one.at[11], chip, core, 1 - head)
    across.start()
    video(6, WITHIN)
    across.wait_recv()
    out[...] = (part[head] + back[...]).astype(BF)

    across.wait_send()
    end_first()
    end_second()
    remote(others, others, one.at[7], one.at[8], chip, 1 - core, head).wait_send()
    send_n.wait_send()
    send_s.wait_send()
    weights = wl.at[pl.ds(0, 2 * GROUP - 1)]
    remote(weights, weights, one.at[0], one.at[1], chip, 1 - core, head).wait_send()
    for j in range(WITHIN):
        pltpu.make_async_copy(os.at[:, lanes(j)], vout.at[:, lanes(j)], pair_out.at[j]).wait()


def main_part(x, w, vclip, aclip, kv, vq, wout):
    n = vq.shape[0]
    dma = pltpu.SemaphoreType.DMA
    return pl.pallas_call(
        main_kernel,
        out_shape=(
            jax.ShapeDtypeStruct((n, 128 * WITHIN), BF),
            jax.ShapeDtypeStruct((256 * (8 - WITHIN), 256), BF),
            jax.ShapeDtypeStruct((32, 128), BF),
        ),
        in_specs=[ANY, VMEM, VMEM, VMEM, ANY, ANY, VMEM],
        out_specs=(ANY, VMEM, VMEM),
        scratch_shapes=[
            pltpu.VMEM((256, 2048), BF),
            pltpu.VMEM((n, 1024), BF),
            pltpu.VMEM((n, 1024), BF),
            pltpu.VMEM((n, 1024), BF),
            pltpu.VMEM((n, 128 * WITHIN), BF),
            pltpu.VMEM((768, 128), BF),
            pltpu.VMEM((16, 48, 128), BF),
            pltpu.VMEM((48, 256), BF),
            pltpu.VMEM((3072, 256), BF),
            pltpu.VMEM((n, 128), BF),
            pltpu.VMEM((256, 128), BF),
            pltpu.VMEM((128, 256), BF),
            pltpu.VMEM((512, n), F32),
            pltpu.VMEM((512, n), F32),
            pltpu.VMEM((512, 128), F32),
            pltpu.VMEM((512, 128), F32),
            pltpu.VMEM((2, 256, 512), F32),
            pltpu.VMEM((2, 256, 128), F32),
            pltpu.VMEM((256, 512), F32),
            pltpu.VMEM((256, 128), F32),
            pltpu.VMEM((CHIPS, 16, 384), BF),
            pltpu.VMEM((CHIPS, 16, 384), BF),
            pltpu.VMEM((16, 256), BF),
            pltpu.VMEM((1024, 256), BF),
            pltpu.VMEM((2, 32, 128), F32),
            pltpu.VMEM((8, 128), F32),
            pltpu.VMEM((32, 128), F32),
            dma((4,)),
            dma((WITHIN,)),
            dma((12,)),
        ]
        + [dma((QUARTERS,))] * 8,
        compiler_params=pltpu.CompilerParams(
            collective_id=0, has_side_effects=True, vmem_limit_bytes=52 * 2**20
        ),
    )(x, w, vclip, aclip, kv, vq, wout)


def tail_kernel(tail, aclip, vclip, vq, first, projected, vout, out, hot, qs, os, sem):
    move = pltpu.make_async_copy(first, vout.at[:, pl.ds(0, 128 * WITHIN)], sem.at[0])
    load = pltpu.make_async_copy(
        vq.at[:, pl.ds(128 * WITHIN, 128 * (8 - WITHIN))], qs, sem.at[1]
    )
    load.start()
    move.start()
    out[...] = projected[...]
    fill_hot(hot, vclip)
    mask_t = clip_mask(aclip).astype(BF)
    load.wait()
    rest = 128 * (8 - WITHIN)
    for j in range(8 - WITHIN):
        at = slice(j * 128, (j + 1) * 128)
        keys, values = tail[at, :], tail[rest + j * 128 : rest + (j + 1) * 128, :]
        video_pair(keys, values, mask_t, hot, qs, os, at)
        pltpu.make_async_copy(
            os.at[:, at], vout.at[:, pl.ds(128 * (WITHIN + j), 128)], sem.at[2 + j]
        ).start()
    for j in range(8 - WITHIN):
        at = slice(j * 128, (j + 1) * 128)
        pltpu.make_async_copy(
            os.at[:, at], vout.at[:, pl.ds(128 * (WITHIN + j), 128)], sem.at[2 + j]
        ).wait()
    move.wait()


def tail_part(tail, aclip, vclip, vq, first, projected):
    n = vq.shape[0]
    return pl.pallas_call(
        tail_kernel,
        out_shape=(jax.ShapeDtypeStruct(vq.shape, BF), jax.ShapeDtypeStruct((32, 128), BF)),
        in_specs=[VMEM, VMEM, VMEM, ANY, ANY, VMEM],
        out_specs=(ANY, VMEM),
        scratch_shapes=[
            pltpu.VMEM((n, 128), BF),
            pltpu.VMEM((n, 128 * (8 - WITHIN)), BF),
            pltpu.VMEM((n, 128 * (8 - WITHIN)), BF),
            pltpu.SemaphoreType.DMA((10 - WITHIN,)),
        ],
        compiler_params=pltpu.CompilerParams(vmem_limit_bytes=40 * 2**20),
    )(tail, aclip, vclip, vq, first, projected)


def shards(vq, kv, video_clip, x, w, audio_clip, wout):
    vclip = video_clip.reshape(-1, 128)
    aclip = audio_clip.reshape(-1, 128)
    first, tail, projected = main_part(x, w, vclip, aclip, kv, vq, wout.T)
    video_attn, out = tail_part(tail, aclip, vclip, vq, first, projected)
    return video_attn, out.T


def solution(mesh):
    return jax.shard_map(
        shards,
        mesh=mesh,
        in_specs=(
            P("seq", "head"),
            P(None, "seq", "head"),
            P("seq"),
            P(),
            P("seq", None, "head"),
            P(),
            P("head", "seq"),
        ),
        out_specs=(P("seq", "head"), P("head", "seq")),
        check_vma=False,
    )
```

```python
import functools

import jax
import jax.numpy as jnp
from jax import lax
from jax.experimental import pallas as pl
from jax.experimental.pallas import tpu as pltpu
from jax.sharding import PartitionSpec as P

F32 = jnp.float32
BF = jnp.bfloat16
NT = (((1,), (1,)), ((), ()))
BIG = -1e30
MESH = pl.DeviceIdType.MESH
VMEM = pl.BlockSpec(memory_space=pltpu.VMEM)
HBM = pl.BlockSpec(memory_space=pltpu.HBM)
CHIPS = 32
GROUP = 8
QUARTERS = 4
DEVICES = 64
SPREAD, UNSPREAD = 3, 43
FIRST = 22
LIMIT = 59 * 2**20
PAIRS = 8
MOVES = 8
SIZE = 512


def lanes(j, width=128):
    return pl.ds(pl.multiple_of(j * width, width), width)


def rows_of(at, n):
    return pl.ds(pl.multiple_of(at, 16), n)


def remote(src, dst, send, recv, chip, core, head):
    return pltpu.make_async_remote_copy(
        src_ref=src,
        dst_ref=dst,
        send_sem=send,
        recv_sem=recv,
        device_id=(chip * 2 + core, head),
        device_id_type=MESH,
    )


def one_hot(clip, count):
    row = lax.broadcasted_iota(jnp.int32, (128, 128), 0)
    return [row == jnp.broadcast_to(clip[t : t + 1, :], (128, 128)) for t in range(count)]


def clip_mask(aclip):
    row = lax.broadcasted_iota(jnp.int32, (128, 128), 0)
    tiles = [jnp.where(same | (row >= 8), 0.0, BIG) for same in one_hot(aclip, 2)]
    return jnp.concatenate(tiles, 1)


def fill_hot(hot, vclip):
    for t, same in enumerate(one_hot(vclip, 16)):
        hot[t * 128 : (t + 1) * 128, :] = jnp.where(same, 1.0, 0.0).T.astype(BF)


def video_pair(kt, vt, mask_t, hot, vq, vout, at):
    size = 1024
    lane = lax.broadcasted_iota(jnp.int32, (size, 128), 1)
    row = lax.broadcasted_iota(jnp.int32, (128, 256), 0)
    scaled = (kt.astype(F32) * 0.125).astype(BF)
    zero = jnp.zeros_like(scaled)
    first = jnp.concatenate([jnp.where(row < 64, scaled, zero), mask_t], 0)
    second = jnp.concatenate([jnp.where(row >= 64, scaled, zero), mask_t], 0)
    keys = jnp.concatenate([first, second], 1)
    values = jnp.concatenate([vt, jnp.ones((128, 256), BF)], 0)
    for c in range(vq.shape[0] // size):
        rows = pl.ds(c * size, size)
        q = jnp.concatenate([vq[rows, at], hot[rows, :]], 1)
        s = jnp.dot(q, keys, preferred_element_type=F32)
        r = []
        for h in range(2):
            sh = s[:, h * 256 : (h + 1) * 256]
            p = jnp.exp(sh - jnp.max(sh, axis=1, keepdims=True)).astype(BF)
            r.append(lax.dot_general(p, values, NT, preferred_element_type=F32))
        num = jnp.where(lane < 64, r[0][:, :128], r[1][:, :128])
        den = jnp.where(lane < 64, r[0][:, 128:], r[1][:, 128:])
        vout[rows, at] = (num / den).astype(BF)


def widened(f, first, count):
    n = f.shape[0]
    lane = lax.broadcasted_iota(jnp.int32, (n, 128), 1)
    out = []
    for p in range(first, first + count, 2):
        a = jnp.broadcast_to(f[:, p : p + 1], (n, 128))
        b = jnp.broadcast_to(f[:, p + 1 : p + 2], (n, 128))
        out.append(jnp.where(lane < 64, a, b))
    return jnp.concatenate(out, 1)


def gather(mine, full, n, send_sem, recv_sem, pass_send, pass_recv, where):
    quarter, g, chip, core, head = where

    def block(q, k, i):
        return full.at[rows_of(((q * 2 + k) * GROUP + i) * n, n)]

    def group(q, k):
        return full.at[rows_of((q * 2 + k) * GROUP * n, GROUP * n)]

    own = block(quarter, core, g)

    def begin():
        pltpu.make_async_copy(mine, own, recv_sem.at[quarter]).start()

        def one(i, _):
            q = lax.rem(quarter + i // GROUP, QUARTERS)
            to = q * GROUP + lax.rem(g + i, GROUP)
            remote(mine, own, send_sem, recv_sem.at[quarter], to, core, head).start()
            return 0

        lax.fori_loop(1, CHIPS, one, 0)

    def relay(q):
        blocks = group(q, core)
        remote(blocks, blocks, send_sem, recv_sem.at[q], chip, 1 - core, head).wait_recv()
        remote(blocks, blocks, pass_send.at[q], pass_recv.at[q], chip, 1 - core, head).start()

    def passed(q):
        blocks = group(q, 1 - core)
        remote(blocks, blocks, pass_send.at[q], pass_recv.at[q], chip, 1 - core, head).wait_recv()

    def end():
        for q in range(QUARTERS):
            blocks = group(q, core)
            remote(
                blocks, blocks, pass_send.at[q], pass_recv.at[q], chip, 1 - core, head
            ).wait_send()
        sent = full.at[pl.ds(0, (CHIPS - 1) * n)]
        remote(sent, sent, send_sem, recv_sem.at[0], chip, 1 - core, head).wait_send()

    return begin, relay, passed, end


def main_kernel(
    x, w, vclip, aclip, kv, vq, wout,
    vout, out,
    ws, xs, vcs, acs, ks, vs, qs, wos, os, wt, wl, mine, qkv, hot, mask, mask_t,
    sa, sb, ma, mb, numer, stat, near_n, near_s, comb, land, attn, gath, part, swap, back,
    local, pair_out, one, bar1, bar2, bar3, bar4, bar5, bar6,
):
    seq, head = lax.axis_index("seq"), lax.axis_index("head")
    chip, core = seq // 2, seq % 2
    quarter, g = chip // GROUP, chip % GROUP
    where = (quarter, g, chip, core, head)

    loads = [
        pltpu.make_async_copy(src, dst, local.at[i])
        for i, (src, dst) in enumerate(
            [(w.at[0], ws), (x, xs), (vclip, vcs), (aclip, acs), (kv.at[0], ks),
             (kv.at[1], vs), (vq, qs), (wout, wos)]
        )
    ]
    load_w, load_x, load_vc, load_ac, load_k, load_v, load_q, load_wo = loads
    load_w.start()
    load_vc.start()
    load_ac.start()
    load_x.start()

    barrier = pltpu.get_barrier_semaphore()

    def greet(i, _):
        to = lax.rem(seq + i, DEVICES)
        pl.semaphore_signal(barrier, inc=1, device_id=(to, head), device_id_type=MESH)
        return 0

    lax.fori_loop(1, DEVICES, greet, 0)
    pl.semaphore_signal(barrier, inc=1, device_id=(seq, 1 - head), device_id_type=MESH)
    load_k.start()
    load_v.start()
    load_q.start()
    load_wo.start()
    load_w.wait()
    wt[...] = ws[...].astype(F32).T.astype(BF)
    pl.semaphore_wait(barrier, DEVICES)

    feature = g * 2 + core
    mine_at = lax.rem(seq * UNSPREAD, DEVICES)
    same_quarter = mine_at // 16 == quarter

    def weights_start(i, _):
        b = lax.rem(feature + i, 16)
        to = lax.rem((quarter * 16 + b) * SPREAD, DEVICES)
        rows = wt.at[rows_of(b * 48, 48)]

        @pl.when(to == seq)
        def _():
            pltpu.make_async_copy(rows, wl.at[feature], one.at[1]).start()

        @pl.when(to != seq)
        def _():
            pltpu.make_async_remote_copy(
                src_ref=rows,
                dst_ref=wl.at[feature],
                send_sem=one.at[0],
                recv_sem=one.at[1],
                device_id=(to, head),
                device_id_type=MESH,
            ).start()

        return 0

    lax.fori_loop(0, 16, weights_start, 0)
    load_vc.wait()
    load_ac.wait()
    fill_hot(hot, vcs)
    flat = clip_mask(acs)
    mask_t[...] = flat.astype(BF)
    mask[...] = flat.T.astype(BF)
    load_x.wait()
    remote(wl, wl, one.at[0], one.at[1], chip, 1 - core, head).wait_recv()
    columns = jnp.concatenate([wl[f] for f in range(16)], 1)
    mine[...] = lax.dot_general(columns, xs[...], NT, preferred_element_type=F32).astype(BF)

    has_query = mine_at < FIRST
    own = qkv.at[rows_of(core * 1536 + mine_at // 2 * 48, 48)]
    spans = ((0, FIRST // 2 * 48), (FIRST // 2 * 48, (32 - FIRST // 2) * 48))

    def span(p, k):
        return qkv.at[rows_of(k * 1536 + spans[p][0], spans[p][1])]

    def begin_first(p):
        pltpu.make_async_copy(mine, own, bar1.at[p]).start()

        def send(i, _):
            to = lax.rem(chip + i, CHIPS)
            remote(mine, own, one.at[2], bar1.at[p], to, core, head).start()
            return 0

        lax.fori_loop(1, CHIPS, send, 0)

    def relay_first(p):
        remote(span(p, core), span(p, core), one.at[2], bar1.at[p], chip, 1 - core, head).wait_recv()
        passing(p, core).start()

    def passing(p, k):
        return remote(span(p, k), span(p, k), bar2.at[p], bar3.at[p], chip, 1 - core, head)

    def end_first():
        passing(0, core).wait_send()
        passing(1, core).wait_send()
        sent = qkv.at[pl.ds(0, (CHIPS - 1) * 48)]
        remote(sent, sent, one.at[2], bar1.at[0], chip, 1 - core, head).wait_send()

    def rows_at(u):
        b = u // 3
        return rows_of(lax.rem(b, 2) * 1536 + b // 2 * 48 + lax.rem(u, 3) * 16, 16)

    def projected(j):
        return jnp.concatenate([qkv[rows_at(8 * j + t), :] for t in range(8)], 0)

    @pl.when(has_query)
    def _():
        begin_first(0)

    relay_first(0)

    @pl.when(jnp.logical_not(has_query))
    def _():
        begin_first(1)

    load_k.wait()
    load_v.wait()
    passing(0, 1 - core).wait_recv()

    pieces = ks.shape[0] // SIZE
    lane = lax.broadcasted_iota(jnp.int32, (256, 128), 1)
    ones = jnp.ones((SIZE, 128), BF)
    stat[...] = jnp.zeros_like(stat)

    def pair_of(jj):
        return lax.rem(jj + 4 * (1 - core), 8)

    def query(jj):
        q = (projected(pair_of(jj)).astype(F32) * 0.125).T
        zero = jnp.zeros_like(q)
        first = jnp.concatenate([jnp.where(lane < 64, q, zero).astype(BF), mask[...]], 1)
        second = jnp.concatenate([jnp.where(lane >= 64, q, zero).astype(BF), mask[...]], 1)
        return jnp.concatenate([first, second], 0)

    def score(jj, q2, c, s_ref, top):
        rows = pl.ds(c * SIZE, SIZE)
        keys = jnp.concatenate([ks[rows, lanes(pair_of(jj))], hot[rows, :]], 1)
        s = lax.dot_general(q2, keys, NT, preferred_element_type=F32)
        s_ref[:, c * SIZE : (c + 1) * SIZE] = s
        for t in range(SIZE // 128):
            piece = s[:, t * 128 : (t + 1) * 128]
            top = piece if top is None else jnp.maximum(top, piece)
        return top

    def keep(top, m_ref):
        m_ref[...] = jnp.broadcast_to(jnp.max(top, axis=1, keepdims=True), (512, 128))

    def weigh(jj, top, c, s_ref, acc):
        rows = pl.ds(c * SIZE, SIZE)
        wide = jnp.concatenate([top] * (SIZE // 128), 1)
        weights = jnp.exp(s_ref[:, c * SIZE : (c + 1) * SIZE] - wide).astype(BF)
        values = jnp.concatenate([vs[rows, lanes(pair_of(jj))], ones], 1)
        r = jnp.dot(weights, values, preferred_element_type=F32)
        return r if acc is None else acc + r

    def step(jj, half, following, s_ref, m_ref, s_next, m_next):
        q2 = query(following)
        top, acc, now = None, None, m_ref[...]
        for c in range(pieces):
            top = score(following, q2, c, s_next, top)
            acc = weigh(jj, now, c, s_ref, acc)
        keep(top, m_next)
        numer[half, :, lanes(jj - 4 * half)] = jnp.where(
            lane < 64, acc[:256, :128], acc[256:, :128]
        )
        st, at = stat[half], 2 * (jj - 4 * half)
        st = jnp.where(lane == at, now[:256], st)
        st = jnp.where(lane == at + 1, now[256:], st)
        st = jnp.where(lane == at + 64, acc[:256, 128:], st)
        stat[half] = jnp.where(lane == at + 65, acc[256:, 128:], st)

    def two(half, i, _):
        jj = 4 * half + 2 * i
        step(jj, half, jj + 1, sa, ma, sb, mb)
        step(jj + 1, half, jnp.minimum(jj + 2, 7), sb, mb, sa, ma)
        return 0

    q2, top = query(0), None
    for c in range(pieces):
        top = score(0, q2, c, sa, top)
    keep(top, ma)
    lax.fori_loop(0, 2, functools.partial(two, 0), 0)
    send_n = remote(numer.at[0], near_n, one.at[3], one.at[4], chip, 1 - core, head)
    send_s = remote(stat.at[0], near_s, one.at[5], one.at[6], chip, 1 - core, head)
    send_n.start()
    send_s.start()
    relay_first(1)
    lax.fori_loop(0, 2, functools.partial(two, 1), 0)

    send_s.wait_recv()
    send_n.wait_recv()
    a, b = stat[1], near_s[...]
    top = jnp.maximum(a, b)
    high = top.astype(BF).astype(F32)
    top = high + (top - high).astype(BF).astype(F32)
    fa = jnp.where(lane < 64, jnp.exp(a - top), 0.0)
    fb = jnp.where(lane < 64, jnp.exp(b - top), 0.0)
    st = jnp.where(lane < 64, top, a * pltpu.roll(fa, 64, 1) + b * pltpu.roll(fb, 64, 1))
    high = st.astype(BF).astype(F32)
    both = numer[1] * widened(fa, 0, 8) + near_n[...] * widened(fb, 0, 8)

    def stacked(u, v):
        return jnp.concatenate(
            [u.reshape(CHIPS, 8, u.shape[1]), v.reshape(CHIPS, 8, v.shape[1])], 1
        ).astype(BF)

    comb[:, :, :256] = stacked(both[:, :256], both[:, 256:])
    comb[:, :, 256:] = stacked(high, st - high)

    def scatter_start(i, _):
        to = lax.rem(chip + i, CHIPS)
        remote(comb.at[to], land.at[i], one.at[7], one.at[8], to, core, head).start()
        return 0

    lax.fori_loop(1, CHIPS, scatter_start, 0)
    land[0] = comb[chip]

    load_q.wait()
    load_wo.wait()
    passing(1, 1 - core).wait_recv()

    def pair_copy(j):
        return pltpu.make_async_copy(os.at[:, lanes(j)], vout.at[:, lanes(j)], pair_out.at[j])

    def video(j0, j1):
        def pair(j, _):
            video_pair(projected(j + 8), projected(j + 16), mask_t[...], hot, qs, os, lanes(j))
            pair_copy(j).start()
            return 0

        lax.fori_loop(j0, j1, pair, 0)

    video(0, 3)

    others = land.at[pl.ds(1, CHIPS - 1)]
    remote(others, others, one.at[7], one.at[8], chip, 1 - core, head).wait_recv()
    arrived = land[:, :, 256:].astype(F32)
    st = arrived[:, :8] + arrived[:, 8:]
    small = lax.broadcasted_iota(jnp.int32, (8, 128), 1)
    top = jnp.max(st, axis=0)
    total = jnp.zeros((16, 256), F32)
    den = jnp.zeros((8, 128), F32)
    for i in range(CHIPS):
        f = jnp.where(small < 64, jnp.exp(st[i] - top), 0.0)
        den = den + st[i] * pltpu.roll(f, 64, 1)
        scale = jnp.concatenate([widened(f, 0, 4), widened(f, 4, 4)], 0)
        total = total + land[i, :, :256].astype(F32) * scale
    scale = jnp.concatenate([widened(den, 64, 4), widened(den, 68, 4)], 0)
    attn[...] = (total / scale).astype(BF)

    begin, relay, passed, end_second = gather(
        attn, gath, 16, one.at[9], bar4, bar5, bar6, where
    )
    begin()
    video(3, 6)
    for q in range(QUARTERS):
        relay(q)
    video(6, 7)
    for q in range(QUARTERS):
        passed(q)
    acc = None
    for k in range(2):
        groups = [
            gath[(q * 2 + k) * GROUP * 16 : (q * 2 + k + 1) * GROUP * 16, :]
            for q in range(QUARTERS)
        ]
        rows = jnp.concatenate(groups, 0)
        for h in range(2):
            at = k * 512 + h * 256
            r = lax.dot_general(rows, wos[:, at : at + 256], NT, preferred_element_type=F32)
            r = r.reshape(CHIPS, 16, 32)[:, h * 8 : (h + 1) * 8]
            acc = r if acc is None else acc + r
    flat = acc.reshape(256, 32).T
    part[0] = flat[:, :128]
    part[1] = flat[:, 128:]
    across = remote(part.at[1 - head], back, one.at[10], one.at[11], chip, core, 1 - head)
    across.start()
    video(7, PAIRS)
    across.wait_recv()
    out[...] = (part[head] + back[...]).astype(BF)

    across.wait_send()
    end_first()
    end_second()
    remote(others, others, one.at[7], one.at[8], chip, 1 - core, head).wait_send()
    send_n.wait_send()
    send_s.wait_send()
    for j in range(PAIRS):
        pair_copy(j).wait()
    for count, holds in ((15, same_quarter), (16, jnp.logical_not(same_quarter))):

        @pl.when(holds)
        def _(count=count):
            weights = wl.at[pl.ds(0, count)]
            remote(weights, weights, one.at[0], one.at[1], chip, 1 - core, head).wait_send()


def main_part(x, w, vclip, aclip, kv, vq, wout):
    n = vq.shape[0]
    dma = pltpu.SemaphoreType.DMA
    return pl.pallas_call(
        main_kernel,
        out_shape=(
            jax.ShapeDtypeStruct((n, 128 * PAIRS), BF),
            jax.ShapeDtypeStruct((32, 128), BF),
        ),
        in_specs=[HBM] * 7,
        out_specs=(HBM, VMEM),
        scratch_shapes=[
            pltpu.VMEM((128, 768), BF),
            pltpu.VMEM((256, 2048), BF),
            pltpu.VMEM((16, 128), jnp.int32),
            pltpu.VMEM((2, 128), jnp.int32),
            pltpu.VMEM((n, 1024), BF),
            pltpu.VMEM((n, 1024), BF),
            pltpu.VMEM((n, 1024), BF),
            pltpu.VMEM((32, 1024), BF),
            pltpu.VMEM((n, 128 * PAIRS), BF),
            pltpu.VMEM((768, 128), BF),
            pltpu.VMEM((16, 48, 128), BF),
            pltpu.VMEM((48, 256), BF),
            pltpu.VMEM((3072, 256), BF),
            pltpu.VMEM((n, 128), BF),
            pltpu.VMEM((256, 128), BF),
            pltpu.VMEM((128, 256), BF),
            pltpu.VMEM((512, n), F32),
            pltpu.VMEM((512, n), F32),
            pltpu.VMEM((512, 128), F32),
            pltpu.VMEM((512, 128), F32),
            pltpu.VMEM((2, 256, 512), F32),
            pltpu.VMEM((2, 256, 128), F32),
            pltpu.VMEM((256, 512), F32),
            pltpu.VMEM((256, 128), F32),
            pltpu.VMEM((CHIPS, 16, 384), BF),
            pltpu.VMEM((CHIPS, 16, 384), BF),
            pltpu.VMEM((16, 256), BF),
            pltpu.VMEM((1024, 256), BF),
            pltpu.VMEM((2, 32, 128), F32),
            pltpu.VMEM((8, 128), F32),
            pltpu.VMEM((32, 128), F32),
            dma((8,)),
            dma((PAIRS,)),
            dma((12,)),
        ]
        + [dma((QUARTERS,))] * 6,
        compiler_params=pltpu.CompilerParams(
            collective_id=0, has_side_effects=True, vmem_limit_bytes=LIMIT
        ),
    )(x, w, vclip, aclip, kv, vq, wout)


def move_kernel(first, projected, vout, out, held, small, read, write, sem):
    n = first.shape[0] // MOVES
    fetch = pltpu.make_async_copy(projected, small, sem.at[0])
    fetch.start()

    def inward(i):
        rows = pl.ds(i * n, n)
        return pltpu.make_async_copy(first.at[rows], held.at[rows], read.at[i])

    def outward(i):
        rows = pl.ds(i * n, n)
        return pltpu.make_async_copy(held.at[rows], vout.at[rows], write.at[i])

    for i in range(MOVES):
        inward(i).start()
    fetch.wait()
    store = pltpu.make_async_copy(small, out, sem.at[1])
    store.start()
    for i in range(MOVES):
        inward(i).wait()
        outward(i).start()
    for i in range(MOVES):
        outward(i).wait()
    store.wait()


def move_part(first, projected):
    dma = pltpu.SemaphoreType.DMA
    return pl.pallas_call(
        move_kernel,
        out_shape=(
            jax.ShapeDtypeStruct(first.shape, BF),
            jax.ShapeDtypeStruct(projected.shape, BF),
        ),
        in_specs=[HBM, HBM],
        out_specs=(HBM, HBM),
        scratch_shapes=[
            pltpu.VMEM(first.shape, BF),
            pltpu.VMEM(projected.shape, BF),
            dma((MOVES,)),
            dma((MOVES,)),
            dma((2,)),
        ],
        compiler_params=pltpu.CompilerParams(vmem_limit_bytes=LIMIT),
    )(first, projected)


def shards(vq, kv, video_clip, x, w, audio_clip, wout):
    vclip = video_clip.reshape(-1, 128)
    aclip = audio_clip.reshape(-1, 128)
    first, projected = main_part(x, w, vclip, aclip, kv, vq, wout.T)
    video_attn, out = move_part(first, projected)
    return video_attn, out.T


def solution(mesh):
    return jax.shard_map(
        shards,
        mesh=mesh,
        in_specs=(
            P("seq", "head"),
            P(None, "seq", "head"),
            P("seq"),
            P(),
            P("seq", None, "head"),
            P(),
            P("head", "seq"),
        ),
        out_specs=(P("seq", "head"), P("head", "seq")),
        check_vma=False,
    )
```

```python
import functools

import jax
import jax.numpy as jnp
from jax import lax
from jax.experimental import pallas as pl
from jax.experimental.pallas import tpu as pltpu
from jax.sharding import PartitionSpec as P

F32 = jnp.float32
BF = jnp.bfloat16
NT = (((1,), (1,)), ((), ()))
BIG = -1e30
MESH = pl.DeviceIdType.MESH
VMEM = pl.BlockSpec(memory_space=pltpu.VMEM)
HBM = pl.BlockSpec(memory_space=pltpu.HBM)
CHIPS = 32
GROUP = 8
QUARTERS = 4
DEVICES = 64
SPREAD, UNSPREAD = 3, 11
FIRST = 11
LIMIT = 59 * 2**20
PAIRS = 8
MOVES = 8
SIZE = 512


def lanes(j, width=128):
    return pl.ds(pl.multiple_of(j * width, width), width)


def rows_of(at, n):
    return pl.ds(pl.multiple_of(at, 16), n)


def remote(src, dst, send, recv, chip, core, head):
    return pltpu.make_async_remote_copy(
        src_ref=src,
        dst_ref=dst,
        send_sem=send,
        recv_sem=recv,
        device_id=(chip * 2 + core, head),
        device_id_type=MESH,
    )


def one_hot(clip, count):
    row = lax.broadcasted_iota(jnp.int32, (128, 128), 0)
    return [row == jnp.broadcast_to(clip[t : t + 1, :], (128, 128)) for t in range(count)]


def clip_mask(aclip):
    row = lax.broadcasted_iota(jnp.int32, (128, 128), 0)
    tiles = [jnp.where(same | (row >= 8), 0.0, BIG) for same in one_hot(aclip, 2)]
    return jnp.concatenate(tiles, 1)


def fill_hot(hot, vclip):
    for t, same in enumerate(one_hot(vclip, 16)):
        hot[t * 128 : (t + 1) * 128, :] = jnp.where(same, 1.0, 0.0).T.astype(BF)


def video_pair(kt, vt, mask_t, hot, vq, vout, at):
    size = 1024
    lane = lax.broadcasted_iota(jnp.int32, (size, 128), 1)
    row = lax.broadcasted_iota(jnp.int32, (128, 256), 0)
    scaled = (kt.astype(F32) * 0.125).astype(BF)
    zero = jnp.zeros_like(scaled)
    first = jnp.concatenate([jnp.where(row < 64, scaled, zero), mask_t], 0)
    second = jnp.concatenate([jnp.where(row >= 64, scaled, zero), mask_t], 0)
    keys = jnp.concatenate([first, second], 1)
    values = jnp.concatenate([vt, jnp.ones((128, 256), BF)], 0)
    for c in range(vq.shape[0] // size):
        rows = pl.ds(c * size, size)
        q = jnp.concatenate([vq[rows, at], hot[rows, :]], 1)
        s = jnp.dot(q, keys, preferred_element_type=F32)
        r = []
        for h in range(2):
            sh = s[:, h * 256 : (h + 1) * 256]
            p = jnp.exp(sh - jnp.max(sh, axis=1, keepdims=True)).astype(BF)
            r.append(lax.dot_general(p, values, NT, preferred_element_type=F32))
        num = jnp.where(lane < 64, r[0][:, :128], r[1][:, :128])
        den = jnp.where(lane < 64, r[0][:, 128:], r[1][:, 128:])
        vout[rows, at] = (num / den).astype(BF)


def widened(f, first, count):
    n = f.shape[0]
    lane = lax.broadcasted_iota(jnp.int32, (n, 128), 1)
    out = []
    for p in range(first, first + count, 2):
        a = jnp.broadcast_to(f[:, p : p + 1], (n, 128))
        b = jnp.broadcast_to(f[:, p + 1 : p + 2], (n, 128))
        out.append(jnp.where(lane < 64, a, b))
    return jnp.concatenate(out, 1)


def main_kernel(
    x, w, vclip, aclip, kv, vq, wout,
    vout, out,
    ws, xs, vcs, acs, ks, vs, qs, wos, os, wt, wl, mine, qkv, hot, mask, mask_t,
    sa, sb, ma, mb, numer, stat, near_n, near_s, comb, land, attn, wide, gath, part, back,
    local, pair_out, one, bar1, bar2, bar3, bar4, last,
):
    seq, head = lax.axis_index("seq"), lax.axis_index("head")
    chip, core = seq // 2, seq % 2
    quarter, g = chip // GROUP, chip % GROUP

    loads = [
        pltpu.make_async_copy(src, dst, local.at[i])
        for i, (src, dst) in enumerate(
            [(w.at[0], ws), (x, xs), (vclip, vcs), (aclip, acs), (kv.at[0], ks),
             (kv.at[1], vs), (vq, qs), (wout, wos)]
        )
    ]
    load_w, load_x, load_vc, load_ac, load_k, load_v, load_q, load_wo = loads
    load_w.start()
    load_vc.start()
    load_ac.start()
    load_x.start()

    barrier = pltpu.get_barrier_semaphore()

    def greet(i, _):
        to = lax.rem(seq + i, DEVICES)
        pl.semaphore_signal(barrier, inc=1, device_id=(to, head), device_id_type=MESH)
        return 0

    lax.fori_loop(1, DEVICES, greet, 0)
    beside = chip * 2 + 1 - core
    for to in (seq, beside):
        pl.semaphore_signal(barrier, inc=1, device_id=(to, 1 - head), device_id_type=MESH)
    load_k.start()
    load_v.start()
    load_q.start()
    load_wo.start()
    load_w.wait()
    wt[...] = ws[...].astype(F32).T.astype(BF)
    pl.semaphore_wait(barrier, DEVICES + 1)

    feature = g * 2 + core
    turn = lax.rem((chip + CHIPS - core) * UNSPREAD, CHIPS)
    late = (turn + CHIPS - FIRST) // CHIPS
    mine_at = (1 - late) * (FIRST * (1 - core) + turn) + late * (FIRST + 21 * core + turn)
    same_quarter = mine_at // 16 == quarter

    def maker(b):
        late = (b + DEVICES - 2 * FIRST) // DEVICES
        k = (1 - late) * (1 - b // FIRST) + late * ((b + 41) // 21 - 3)
        turn = (1 - late) * (b % FIRST) + late * (FIRST + (b + 41) % 21)
        return lax.rem(turn * SPREAD + k, CHIPS) * 2 + k

    def weights_start(i, _):
        b = lax.rem(feature + i, 16)
        to = maker(quarter * 16 + b)
        rows = wt.at[rows_of(b * 48, 48)]

        @pl.when(to == seq)
        def _():
            pltpu.make_async_copy(rows, wl.at[feature], one.at[1]).start()

        @pl.when(to != seq)
        def _():
            pltpu.make_async_remote_copy(
                src_ref=rows,
                dst_ref=wl.at[feature],
                send_sem=one.at[0],
                recv_sem=one.at[1],
                device_id=(to, head),
                device_id_type=MESH,
            ).start()

        return 0

    lax.fori_loop(0, 16, weights_start, 0)
    load_wo.wait()
    swap_w = remote(
        wos.at[:, lanes(1 - core, 512)], wide.at[pl.ds(32, 32)], last.at[0], last.at[1],
        chip, 1 - core, head,
    )
    swap_w.start()
    wide[:32, :] = wos[:, lanes(core, 512)]
    load_vc.wait()
    load_ac.wait()
    fill_hot(hot, vcs)
    flat = clip_mask(acs)
    mask_t[...] = flat.astype(BF)
    mask[...] = flat.T.astype(BF)
    load_x.wait()
    remote(wl, wl, one.at[0], one.at[1], chip, 1 - core, head).wait_recv()
    columns = jnp.concatenate([wl[f] for f in range(16)], 1)
    mine[...] = lax.dot_general(columns, xs[...], NT, preferred_element_type=F32).astype(BF)

    has_query = turn < FIRST
    own = qkv.at[rows_of(mine_at * 48, 48)]

    def span(k):
        return qkv.at[rows_of((2 * FIRST + 21 * k) * 48, 21 * 48)]

    def query_block(k, i):
        return qkv.at[rows_of((FIRST * (1 - k) + i) * 48, 48)]

    def begin_first(sem):
        pltpu.make_async_copy(mine, own, sem).start()

        def send(i, _):
            to = lax.rem(chip + i, CHIPS)
            remote(mine, own, one.at[2], sem, to, core, head).start()
            return 0

        lax.fori_loop(1, CHIPS, send, 0)

    def passing_query(k, i):
        block = query_block(k, i)
        return remote(block, block, bar2.at[i], bar3.at[i], chip, 1 - core, head)

    def relay_query(n, _):
        i = lax.rem(n + chip, FIRST)
        block = query_block(core, i)
        remote(block, block, one.at[2], bar1.at[i], chip, 1 - core, head).wait_recv()
        passing_query(core, i).start()
        return 0

    def query_passed(i, _):
        passing_query(1 - core, i).wait_recv()
        return 0

    def passing(k):
        return remote(span(k), span(k), bar2.at[FIRST], bar3.at[FIRST], chip, 1 - core, head)

    def relay_rest():
        remote(span(core), span(core), one.at[2], bar1.at[FIRST], chip, 1 - core, head).wait_recv()
        passing(core).start()

    def end_first():
        def query_sent(i, _):
            passing_query(core, i).wait_send()
            return 0

        lax.fori_loop(0, FIRST, query_sent, 0)
        passing(core).wait_send()
        sent = qkv.at[pl.ds(0, (CHIPS - 1) * 48)]
        remote(sent, sent, one.at[2], bar1.at[FIRST], chip, 1 - core, head).wait_send()

    def projected(j):
        return qkv[lanes(j), :]

    @pl.when(has_query)
    def _():
        begin_first(bar1.at[turn])

    lax.fori_loop(0, FIRST, relay_query, 0)

    @pl.when(jnp.logical_not(has_query))
    def _():
        begin_first(bar1.at[FIRST])

    load_k.wait()
    load_v.wait()

    pieces = ks.shape[0] // SIZE
    lane = lax.broadcasted_iota(jnp.int32, (256, 128), 1)
    ones = jnp.ones((SIZE, 128), BF)
    stat[...] = jnp.zeros_like(stat)

    def within(jj):
        return (jj % 4 + (1 - jj // 4) * (1 - core)) % 4

    def pair_of(jj):
        half = jj // 4
        return 4 * ((1 - core) * (1 - half) + core * half) + within(jj)

    def query(jj):
        q = (projected(pair_of(jj)).astype(F32) * 0.125).T
        zero = jnp.zeros_like(q)
        first = jnp.concatenate([jnp.where(lane < 64, q, zero).astype(BF), mask[...]], 1)
        second = jnp.concatenate([jnp.where(lane >= 64, q, zero).astype(BF), mask[...]], 1)
        return jnp.concatenate([first, second], 0)

    def score(jj, q2, c, s_ref, top):
        rows = pl.ds(c * SIZE, SIZE)
        keys = jnp.concatenate([ks[rows, lanes(pair_of(jj))], hot[rows, :]], 1)
        s = lax.dot_general(q2, keys, NT, preferred_element_type=F32)
        s_ref[:, c * SIZE : (c + 1) * SIZE] = s
        for t in range(SIZE // 128):
            piece = s[:, t * 128 : (t + 1) * 128]
            top = piece if top is None else jnp.maximum(top, piece)
        return top

    def keep(top, m_ref):
        m_ref[...] = jnp.broadcast_to(jnp.max(top, axis=1, keepdims=True), (512, 128))

    def weigh(jj, top, c, s_ref, acc):
        rows = pl.ds(c * SIZE, SIZE)
        wide = jnp.concatenate([top] * (SIZE // 128), 1)
        weights = jnp.exp(s_ref[:, c * SIZE : (c + 1) * SIZE] - wide).astype(BF)
        values = jnp.concatenate([vs[rows, lanes(pair_of(jj))], ones], 1)
        r = jnp.dot(weights, values, preferred_element_type=F32)
        return r if acc is None else acc + r

    def step(jj, half, following, s_ref, m_ref, s_next, m_next):
        top, acc, now = None, None, m_ref[...]
        if following is not None:
            q2 = query(following)
        for c in range(pieces):
            if following is not None:
                top = score(following, q2, c, s_next, top)
            acc = weigh(jj, now, c, s_ref, acc)
        if following is not None:
            keep(top, m_next)
        numer[half, :, lanes(within(jj))] = jnp.where(
            lane < 64, acc[:256, :128], acc[256:, :128]
        )
        st, at = stat[half], 2 * within(jj)
        st = jnp.where(lane == at, now[:256], st)
        st = jnp.where(lane == at + 1, now[256:], st)
        st = jnp.where(lane == at + 64, acc[:256, 128:], st)
        stat[half] = jnp.where(lane == at + 65, acc[256:, 128:], st)

    def two(half, i, _):
        jj = 4 * half + 2 * i
        step(jj, half, jj + 1, sa, ma, sb, mb)
        step(jj + 1, half, jj + 2, sb, mb, sa, ma)

        @pl.when(jj == 0)
        def _():
            lax.fori_loop(0, FIRST, query_passed, 0)

        return 0

    q2, top = query(0), None
    for c in range(pieces):
        top = score(0, q2, c, sa, top)
    keep(top, ma)
    lax.fori_loop(0, 2, functools.partial(two, 0), 0)
    send_n = remote(numer.at[0], near_n, one.at[3], one.at[4], chip, 1 - core, head)
    send_s = remote(stat.at[0], near_s, one.at[5], one.at[6], chip, 1 - core, head)
    send_n.start()
    send_s.start()
    two(1, 0, 0)
    step(6, 1, 7, sa, ma, sb, mb)
    step(7, 1, None, sb, mb, None, None)
    relay_rest()

    send_s.wait_recv()
    send_n.wait_recv()
    narrow = lax.broadcasted_iota(jnp.int32, (64, 128), 1)

    def stacked(u, v):
        u, v = u.reshape(GROUP, 8, u.shape[1]), v.reshape(GROUP, 8, v.shape[1])
        return jnp.concatenate([u, v], 1).astype(BF)

    def combine(c, _):
        base = lax.rem(quarter + 1 + c, QUARTERS) * GROUP
        rows = rows_of(base * 8, 64)
        a, b = stat[1, rows, :], near_s[rows, :]
        top = jnp.maximum(a, b)
        high = top.astype(BF).astype(F32)
        top = high + (top - high).astype(BF).astype(F32)
        fa = jnp.where(narrow < 64, jnp.exp(a - top), 0.0)
        fb = jnp.where(narrow < 64, jnp.exp(b - top), 0.0)
        st = jnp.where(narrow < 64, top, a * pltpu.roll(fa, 64, 1) + b * pltpu.roll(fb, 64, 1))
        high = st.astype(BF).astype(F32)
        both = numer[1, rows, :] * widened(fa, 0, 8) + near_n[rows, :] * widened(fb, 0, 8)
        chips = pl.ds(base, GROUP)
        comb[chips, :, :256] = stacked(both[:, :256], both[:, 256:])
        comb[chips, :, 256:] = stacked(high, st - high)

        def send(i, _):
            to = base + lax.rem(g + i, GROUP)

            @pl.when(to != chip)
            def _():
                slot = lax.rem(to - chip + CHIPS, CHIPS)
                remote(comb.at[to], land.at[slot], one.at[7], one.at[8], to, core, head).start()

            return 0

        lax.fori_loop(0, GROUP, send, 0)
        return 0

    lax.fori_loop(0, QUARTERS, combine, 0)
    land[0] = comb[chip]

    load_q.wait()
    passing(1 - core).wait_recv()

    def pair_copy(j):
        return pltpu.make_async_copy(os.at[:, lanes(j)], vout.at[:, lanes(j)], pair_out.at[j])

    def video(j0, j1):
        def pair(j, _):
            video_pair(projected(j + 8), projected(j + 16), mask_t[...], hot, qs, os, lanes(j))
            pair_copy(j).start()
            return 0

        lax.fori_loop(j0, j1, pair, 0)

    video(0, 4)

    others = land.at[pl.ds(1, CHIPS - 1)]
    remote(others, others, one.at[7], one.at[8], chip, 1 - core, head).wait_recv()
    arrived = land[:, :, 256:].astype(F32)
    st = arrived[:, :8] + arrived[:, 8:]
    small = lax.broadcasted_iota(jnp.int32, (8, 128), 1)
    top = jnp.max(st, axis=0)
    total = jnp.zeros((16, 256), F32)
    den = jnp.zeros((8, 128), F32)
    for i in range(CHIPS):
        f = jnp.where(small < 64, jnp.exp(st[i] - top), 0.0)
        den = den + st[i] * pltpu.roll(f, 64, 1)
        scale = jnp.concatenate([widened(f, 0, 4), widened(f, 4, 4)], 0)
        total = total + land[i, :, :256].astype(F32) * scale
    scale = jnp.concatenate([widened(den, 64, 4), widened(den, 68, 4)], 0)
    attn[...] = (total / scale).astype(BF)

    block = gath.at[rows_of(chip * 16, 16)]
    pltpu.make_async_copy(attn, block, bar4.at[0]).start()

    def attn_start(i, _):
        to = lax.rem(chip + i, CHIPS)
        remote(attn, block, one.at[9], bar4.at[0], to, core, head).start()
        return 0

    lax.fori_loop(1, CHIPS, attn_start, 0)
    video(4, 7)
    remote(gath, gath, one.at[9], bar4.at[0], chip, 1 - core, head).wait_recv()
    swap_w.wait_recv()
    acc = None
    for h in range(2):
        weights = wide[:, h * 256 : (h + 1) * 256]
        r = lax.dot_general(gath[...], weights, NT, preferred_element_type=F32)
        r = r.reshape(CHIPS, 16, 64)[:, h * 8 : (h + 1) * 8]
        acc = r if acc is None else acc + r
    flat = acc.reshape(256, 64).T
    for k in range(2):
        for h in range(2):
            part[k, h] = flat[k * 32 : (k + 1) * 32, h * 128 : (h + 1) * 128]
    across = [
        remote(part.at[1, head], back.at[0], last.at[2], last.at[3], chip, 1 - core, head),
        remote(part.at[0, 1 - head], back.at[1], last.at[4], last.at[5], chip, core, 1 - head),
        remote(part.at[1, 1 - head], back.at[2], last.at[6], last.at[7], chip, 1 - core, 1 - head),
    ]
    for copy in across:
        copy.start()
    video(7, PAIRS)
    total = part[0, head]
    for i, copy in enumerate(across):
        copy.wait_recv()
        total = total + back[i]
    out[...] = total.astype(BF)

    for copy in across:
        copy.wait_send()
    swap_w.wait_send()
    end_first()
    most = gath.at[pl.ds(0, (CHIPS - 1) * 16)]
    remote(most, most, one.at[9], bar4.at[0], chip, 1 - core, head).wait_send()
    remote(others, others, one.at[7], one.at[8], chip, 1 - core, head).wait_send()
    send_n.wait_send()
    send_s.wait_send()
    for j in range(PAIRS):
        pair_copy(j).wait()
    for count, holds in ((15, same_quarter), (16, jnp.logical_not(same_quarter))):

        @pl.when(holds)
        def _(count=count):
            weights = wl.at[pl.ds(0, count)]
            remote(weights, weights, one.at[0], one.at[1], chip, 1 - core, head).wait_send()


def main_part(x, w, vclip, aclip, kv, vq, wout):
    n = vq.shape[0]
    dma = pltpu.SemaphoreType.DMA
    return pl.pallas_call(
        main_kernel,
        out_shape=(
            jax.ShapeDtypeStruct((n, 128 * PAIRS), BF),
            jax.ShapeDtypeStruct((32, 128), BF),
        ),
        in_specs=[HBM] * 7,
        out_specs=(HBM, VMEM),
        scratch_shapes=[
            pltpu.VMEM((128, 768), BF),
            pltpu.VMEM((256, 2048), BF),
            pltpu.VMEM((16, 128), jnp.int32),
            pltpu.VMEM((2, 128), jnp.int32),
            pltpu.VMEM((n, 1024), BF),
            pltpu.VMEM((n, 1024), BF),
            pltpu.VMEM((n, 1024), BF),
            pltpu.VMEM((32, 1024), BF),
            pltpu.VMEM((n, 128 * PAIRS), BF),
            pltpu.VMEM((768, 128), BF),
            pltpu.VMEM((16, 48, 128), BF),
            pltpu.VMEM((48, 256), BF),
            pltpu.VMEM((3072, 256), BF),
            pltpu.VMEM((n, 128), BF),
            pltpu.VMEM((256, 128), BF),
            pltpu.VMEM((128, 256), BF),
            pltpu.VMEM((512, n), F32),
            pltpu.VMEM((512, n), F32),
            pltpu.VMEM((512, 128), F32),
            pltpu.VMEM((512, 128), F32),
            pltpu.VMEM((2, 256, 512), F32),
            pltpu.VMEM((2, 256, 128), F32),
            pltpu.VMEM((256, 512), F32),
            pltpu.VMEM((256, 128), F32),
            pltpu.VMEM((CHIPS, 16, 384), BF),
            pltpu.VMEM((CHIPS, 16, 384), BF),
            pltpu.VMEM((16, 256), BF),
            pltpu.VMEM((64, 512), BF),
            pltpu.VMEM((CHIPS * 16, 256), BF),
            pltpu.VMEM((2, 2, 32, 128), F32),
            pltpu.VMEM((3, 32, 128), F32),
            dma((8,)),
            dma((PAIRS,)),
            dma((12,)),
        ]
        + [dma((FIRST + 1,))] * 3
        + [dma((1,)), dma((8,))],
        compiler_params=pltpu.CompilerParams(
            collective_id=0, has_side_effects=True, vmem_limit_bytes=LIMIT
        ),
    )(x, w, vclip, aclip, kv, vq, wout)


def move_kernel(first, projected, vout, out, held, small, read, write, sem):
    n = first.shape[0] // MOVES
    fetch = pltpu.make_async_copy(projected, small, sem.at[0])
    fetch.start()

    def inward(i):
        rows = pl.ds(i * n, n)
        return pltpu.make_async_copy(first.at[rows], held.at[rows], read.at[i])

    def outward(i):
        rows = pl.ds(i * n, n)
        return pltpu.make_async_copy(held.at[rows], vout.at[rows], write.at[i])

    for i in range(MOVES):
        inward(i).start()
    fetch.wait()
    store = pltpu.make_async_copy(small, out, sem.at[1])
    store.start()
    for i in range(MOVES):
        inward(i).wait()
        outward(i).start()
    for i in range(MOVES):
        outward(i).wait()
    store.wait()


def move_part(first, projected):
    dma = pltpu.SemaphoreType.DMA
    return pl.pallas_call(
        move_kernel,
        out_shape=(
            jax.ShapeDtypeStruct(first.shape, BF),
            jax.ShapeDtypeStruct(projected.shape, BF),
        ),
        in_specs=[HBM, HBM],
        out_specs=(HBM, HBM),
        scratch_shapes=[
            pltpu.VMEM(first.shape, BF),
            pltpu.VMEM(projected.shape, BF),
            dma((MOVES,)),
            dma((MOVES,)),
            dma((2,)),
        ],
        compiler_params=pltpu.CompilerParams(vmem_limit_bytes=LIMIT),
    )(first, projected)


def shards(vq, kv, video_clip, x, w, audio_clip, wout):
    vclip = video_clip.reshape(-1, 128)
    aclip = audio_clip.reshape(-1, 128)
    first, projected = main_part(x, w, vclip, aclip, kv, vq, wout.T)
    video_attn, out = move_part(first, projected)
    return video_attn, out.T


def solution(mesh):
    return jax.shard_map(
        shards,
        mesh=mesh,
        in_specs=(
            P("seq", "head"),
            P(None, "seq", "head"),
            P("seq"),
            P(),
            P("seq", None, "head"),
            P(),
            P("head", "seq"),
        ),
        out_specs=(P("seq", "head"), P("head", "seq")),
        check_vma=False,
    )
```

```python
import functools

import jax
import jax.numpy as jnp
from jax import lax
from jax.experimental import pallas as pl
from jax.experimental.pallas import tpu as pltpu
from jax.sharding import PartitionSpec as P

F32 = jnp.float32
BF = jnp.bfloat16
NT = (((1,), (1,)), ((), ()))
BIG = -1e30
MESH = pl.DeviceIdType.MESH
VMEM = pl.BlockSpec(memory_space=pltpu.VMEM)
HBM = pl.BlockSpec(memory_space=pltpu.HBM)
CHIPS = 32
GROUP = 8
QUARTERS = 4
DEVICES = 64
SPREAD, UNSPREAD = 3, 11
FIRST = 11
LIMIT = 59 * 2**20
PAIRS = 8
MOVES = 8
SIZE = 512


def lanes(j, width=128):
    return pl.ds(pl.multiple_of(j * width, width), width)


def rows_of(at, n):
    return pl.ds(pl.multiple_of(at, 16), n)


def remote(src, dst, send, recv, chip, core, head):
    return pltpu.make_async_remote_copy(
        src_ref=src,
        dst_ref=dst,
        send_sem=send,
        recv_sem=recv,
        device_id=(chip * 2 + core, head),
        device_id_type=MESH,
    )


def one_hot(clip, count):
    row = lax.broadcasted_iota(jnp.int32, (128, 128), 0)
    return [row == jnp.broadcast_to(clip[t : t + 1, :], (128, 128)) for t in range(count)]


def clip_mask(aclip):
    row = lax.broadcasted_iota(jnp.int32, (128, 128), 0)
    tiles = [jnp.where(same | (row >= 8), 0.0, BIG) for same in one_hot(aclip, 2)]
    return jnp.concatenate(tiles, 1)


def fill_hot(hot, vclip):
    for t, same in enumerate(one_hot(vclip, 16)):
        hot[t * 128 : (t + 1) * 128, :] = jnp.where(same, 1.0, 0.0).T.astype(BF)


def video_pair(kt, vt, mask_t, hot, vq, vout, at):
    size = 1024
    lane = lax.broadcasted_iota(jnp.int32, (size, 128), 1)
    row = lax.broadcasted_iota(jnp.int32, (128, 256), 0)
    scaled = (kt.astype(F32) * 0.125).astype(BF)
    zero = jnp.zeros_like(scaled)
    first = jnp.concatenate([jnp.where(row < 64, scaled, zero), mask_t], 0)
    second = jnp.concatenate([jnp.where(row >= 64, scaled, zero), mask_t], 0)
    keys = jnp.concatenate([first, second], 1)
    values = jnp.concatenate([vt, jnp.ones((128, 256), BF)], 0)
    for c in range(vq.shape[0] // size):
        rows = pl.ds(c * size, size)
        q = jnp.concatenate([vq[rows, at], hot[rows, :]], 1)
        s = jnp.dot(q, keys, preferred_element_type=F32)
        r = []
        for h in range(2):
            sh = s[:, h * 256 : (h + 1) * 256]
            p = jnp.exp(sh - jnp.max(sh, axis=1, keepdims=True)).astype(BF)
            r.append(lax.dot_general(p, values, NT, preferred_element_type=F32))
        num = jnp.where(lane < 64, r[0][:, :128], r[1][:, :128])
        den = jnp.where(lane < 64, r[0][:, 128:], r[1][:, 128:])
        vout[rows, at] = (num / den).astype(BF)


def widened(f, first, count):
    n = f.shape[0]
    lane = lax.broadcasted_iota(jnp.int32, (n, 128), 1)
    out = []
    for p in range(first, first + count, 2):
        a = jnp.broadcast_to(f[:, p : p + 1], (n, 128))
        b = jnp.broadcast_to(f[:, p + 1 : p + 2], (n, 128))
        out.append(jnp.where(lane < 64, a, b))
    return jnp.concatenate(out, 1)


def main_kernel(
    x, w, vclip, aclip, kv, vq, wout,
    vout, out,
    ws, xs, vcs, acs, ks, vs, qs, wos, os, wt, wl, mine, qkv, hot, mask, mask_t,
    sa, sb, ma, mb, numer, stat, near_n, near_s, comb, land, attn, wide, gath, part, back,
    local, pair_out, one, bar1, bar2, bar3, bar4, last,
):
    seq, head = lax.axis_index("seq"), lax.axis_index("head")
    chip, core = seq // 2, seq % 2
    quarter, g = chip // GROUP, chip % GROUP

    loads = [
        pltpu.make_async_copy(src, dst, local.at[i])
        for i, (src, dst) in enumerate(
            [(w.at[0], ws), (x, xs), (vclip, vcs), (aclip, acs), (kv.at[0], ks),
             (kv.at[1], vs), (vq, qs), (wout, wos)]
        )
    ]
    load_w, load_x, load_vc, load_ac, load_k, load_v, load_q, load_wo = loads
    load_w.start()
    load_vc.start()
    load_ac.start()
    load_x.start()

    barrier = pltpu.get_barrier_semaphore()

    def greet(i, _):
        to = lax.rem(seq + i, DEVICES)
        pl.semaphore_signal(barrier, inc=1, device_id=(to, head), device_id_type=MESH)
        return 0

    lax.fori_loop(1, DEVICES, greet, 0)
    beside = chip * 2 + 1 - core
    for to in (seq, beside):
        pl.semaphore_signal(barrier, inc=1, device_id=(to, 1 - head), device_id_type=MESH)
    load_k.start()
    load_v.start()
    load_q.start()
    load_wo.start()
    load_w.wait()
    wt[...] = ws[...].astype(F32).T.astype(BF)
    pl.semaphore_wait(barrier, DEVICES + 1)

    feature = g * 2 + core
    turn = lax.rem((chip + CHIPS - core) * UNSPREAD, CHIPS)
    late = (turn + CHIPS - FIRST) // CHIPS
    mine_at = (1 - late) * (FIRST * (1 - core) + turn) + late * (FIRST + 21 * core + turn)
    same_quarter = mine_at // 16 == quarter

    def maker(b):
        late = (b + DEVICES - 2 * FIRST) // DEVICES
        k = (1 - late) * (1 - b // FIRST) + late * ((b + 41) // 21 - 3)
        turn = (1 - late) * (b % FIRST) + late * (FIRST + (b + 41) % 21)
        return lax.rem(turn * SPREAD + k, CHIPS) * 2 + k

    def weights_start(i, _):
        b = lax.rem(feature + i, 16)
        to = maker(quarter * 16 + b)
        rows = wt.at[rows_of(b * 48, 48)]

        @pl.when(to == seq)
        def _():
            pltpu.make_async_copy(rows, wl.at[feature], one.at[1]).start()

        @pl.when(to != seq)
        def _():
            pltpu.make_async_remote_copy(
                src_ref=rows,
                dst_ref=wl.at[feature],
                send_sem=one.at[0],
                recv_sem=one.at[1],
                device_id=(to, head),
                device_id_type=MESH,
            ).start()

        return 0

    lax.fori_loop(0, 16, weights_start, 0)
    load_wo.wait()
    swap_w = remote(
        wos.at[:, lanes(1 - core, 512)], wide.at[pl.ds(32, 32)], last.at[0], last.at[1],
        chip, 1 - core, head,
    )
    swap_w.start()
    wide[:32, :] = wos[:, lanes(core, 512)]
    load_vc.wait()
    load_ac.wait()
    fill_hot(hot, vcs)
    flat = clip_mask(acs)
    mask_t[...] = flat.astype(BF)
    mask[...] = flat.T.astype(BF)
    load_x.wait()
    remote(wl, wl, one.at[0], one.at[1], chip, 1 - core, head).wait_recv()
    columns = jnp.concatenate([wl[f] for f in range(16)], 1)
    mine[...] = lax.dot_general(columns, xs[...], NT, preferred_element_type=F32).astype(BF)

    has_query = turn < FIRST
    own = qkv.at[rows_of(mine_at * 48, 48)]

    def span(k):
        return qkv.at[rows_of((2 * FIRST + 21 * k) * 48, 21 * 48)]

    def query_block(k, i):
        return qkv.at[rows_of((FIRST * (1 - k) + i) * 48, 48)]

    def begin_first(sem):
        pltpu.make_async_copy(mine, own, sem).start()

        def send(i, _):
            to = lax.rem(chip + i, CHIPS)
            remote(mine, own, one.at[2], sem, to, core, head).start()
            return 0

        lax.fori_loop(1, CHIPS, send, 0)

    def passing_query(k, i):
        block = query_block(k, i)
        return remote(block, block, bar2.at[i], bar3.at[i], chip, 1 - core, head)

    def relay_query(n, _):
        i = lax.rem(n + chip, FIRST)
        block = query_block(core, i)
        remote(block, block, one.at[2], bar1.at[i], chip, 1 - core, head).wait_recv()
        passing_query(core, i).start()
        return 0

    def query_passed(i, _):
        passing_query(1 - core, i).wait_recv()
        return 0

    def passing(k):
        return remote(span(k), span(k), bar2.at[FIRST], bar3.at[FIRST], chip, 1 - core, head)

    def relay_rest():
        remote(span(core), span(core), one.at[2], bar1.at[FIRST], chip, 1 - core, head).wait_recv()
        passing(core).start()

    def end_first():
        def query_sent(i, _):
            passing_query(core, i).wait_send()
            return 0

        lax.fori_loop(0, FIRST, query_sent, 0)
        passing(core).wait_send()
        sent = qkv.at[pl.ds(0, (CHIPS - 1) * 48)]
        remote(sent, sent, one.at[2], bar1.at[FIRST], chip, 1 - core, head).wait_send()

    def projected(j):
        return qkv[lanes(j), :]

    @pl.when(has_query)
    def _():
        begin_first(bar1.at[turn])

    lax.fori_loop(0, FIRST, relay_query, 0)

    @pl.when(jnp.logical_not(has_query))
    def _():
        begin_first(bar1.at[FIRST])

    load_k.wait()
    load_v.wait()

    pieces = ks.shape[0] // SIZE
    lane = lax.broadcasted_iota(jnp.int32, (256, 128), 1)
    ones = jnp.ones((SIZE, 128), BF)
    stat[...] = jnp.zeros_like(stat)

    def within(jj):
        return (jj % 4 + (1 - jj // 4) * (1 - core)) % 4

    def pair_of(jj):
        half = jj // 4
        return 4 * ((1 - core) * (1 - half) + core * half) + within(jj)

    def query(jj):
        q = (projected(pair_of(jj)).astype(F32) * 0.125).T
        zero = jnp.zeros_like(q)
        first = jnp.concatenate([jnp.where(lane < 64, q, zero).astype(BF), mask[...]], 1)
        second = jnp.concatenate([jnp.where(lane >= 64, q, zero).astype(BF), mask[...]], 1)
        return jnp.concatenate([first, second], 0)

    def score(jj, q2, c, s_ref, top):
        rows = pl.ds(c * SIZE, SIZE)
        keys = jnp.concatenate([ks[rows, lanes(pair_of(jj))], hot[rows, :]], 1)
        s = lax.dot_general(q2, keys, NT, preferred_element_type=F32)
        s_ref[:, c * SIZE : (c + 1) * SIZE] = s
        for t in range(SIZE // 128):
            piece = s[:, t * 128 : (t + 1) * 128]
            top = piece if top is None else jnp.maximum(top, piece)
        return top

    def keep(top, m_ref):
        m_ref[...] = jnp.broadcast_to(jnp.max(top, axis=1, keepdims=True), (512, 128))

    def weigh(jj, top, c, s_ref, acc):
        rows = pl.ds(c * SIZE, SIZE)
        wide = jnp.concatenate([top] * (SIZE // 128), 1)
        weights = jnp.exp(s_ref[:, c * SIZE : (c + 1) * SIZE] - wide).astype(BF)
        values = jnp.concatenate([vs[rows, lanes(pair_of(jj))], ones], 1)
        r = jnp.dot(weights, values, preferred_element_type=F32)
        return r if acc is None else acc + r

    def step(jj, half, following, s_ref, m_ref, s_next, m_next):
        top, acc, now = None, None, m_ref[...]
        if following is not None:
            q2 = query(following)
        for c in range(pieces):
            if following is not None:
                top = score(following, q2, c, s_next, top)
            acc = weigh(jj, now, c, s_ref, acc)
        if following is not None:
            keep(top, m_next)
        numer[half, :, lanes(within(jj))] = jnp.where(
            lane < 64, acc[:256, :128], acc[256:, :128]
        )
        st, at = stat[half], 2 * within(jj)
        st = jnp.where(lane == at, now[:256], st)
        st = jnp.where(lane == at + 1, now[256:], st)
        st = jnp.where(lane == at + 64, acc[:256, 128:], st)
        stat[half] = jnp.where(lane == at + 65, acc[256:, 128:], st)

    def two(half, i, _):
        jj = 4 * half + 2 * i
        step(jj, half, jj + 1, sa, ma, sb, mb)
        step(jj + 1, half, jj + 2, sb, mb, sa, ma)

        @pl.when(jj == 0)
        def _():
            lax.fori_loop(0, FIRST, query_passed, 0)

        return 0

    q2, top = query(0), None
    for c in range(pieces):
        top = score(0, q2, c, sa, top)
    keep(top, ma)
    lax.fori_loop(0, 2, functools.partial(two, 0), 0)
    send_n = remote(numer.at[0], near_n, one.at[3], one.at[4], chip, 1 - core, head)
    send_s = remote(stat.at[0], near_s, one.at[5], one.at[6], chip, 1 - core, head)
    send_n.start()
    send_s.start()
    two(1, 0, 0)
    step(6, 1, 7, sa, ma, sb, mb)
    step(7, 1, None, sb, mb, None, None)
    relay_rest()

    send_s.wait_recv()
    send_n.wait_recv()
    narrow = lax.broadcasted_iota(jnp.int32, (64, 128), 1)

    def stacked(u, v):
        u, v = u.reshape(GROUP, 8, u.shape[1]), v.reshape(GROUP, 8, v.shape[1])
        return jnp.concatenate([u, v], 1).astype(BF)

    def combine(c, _):
        base = lax.rem(quarter + 1 + c, QUARTERS) * GROUP
        rows = rows_of(base * 8, 64)
        a, b = stat[1, rows, :], near_s[rows, :]
        top = jnp.maximum(a, b)
        high = top.astype(BF).astype(F32)
        top = high + (top - high).astype(BF).astype(F32)
        fa = jnp.where(narrow < 64, jnp.exp(a - top), 0.0)
        fb = jnp.where(narrow < 64, jnp.exp(b - top), 0.0)
        st = jnp.where(narrow < 64, top, a * pltpu.roll(fa, 64, 1) + b * pltpu.roll(fb, 64, 1))
        high = st.astype(BF).astype(F32)
        both = numer[1, rows, :] * widened(fa, 0, 8) + near_n[rows, :] * widened(fb, 0, 8)
        chips = pl.ds(base, GROUP)
        comb[chips, :, :256] = stacked(both[:, :256], both[:, 256:])
        comb[chips, :, 256:] = stacked(high, st - high)

        def send(i, _):
            to = base + lax.rem(g + i, GROUP)

            @pl.when(to != chip)
            def _():
                slot = lax.rem(to - chip + CHIPS, CHIPS)
                remote(comb.at[to], land.at[slot], one.at[7], one.at[8], to, core, head).start()

            return 0

        lax.fori_loop(0, GROUP, send, 0)
        return 0

    lax.fori_loop(0, QUARTERS, combine, 0)
    land[0] = comb[chip]

    load_q.wait()
    passing(1 - core).wait_recv()

    def pair_copy(j):
        return pltpu.make_async_copy(os.at[:, lanes(j)], vout.at[:, lanes(j)], pair_out.at[j])

    def video(j0, j1):
        def pair(j, _):
            video_pair(projected(j + 8), projected(j + 16), mask_t[...], hot, qs, os, lanes(j))
            pair_copy(j).start()
            return 0

        lax.fori_loop(j0, j1, pair, 0)

    video(0, 3)

    others = land.at[pl.ds(1, CHIPS - 1)]
    remote(others, others, one.at[7], one.at[8], chip, 1 - core, head).wait_recv()
    arrived = land[:, :, 256:].astype(F32)
    st = arrived[:, :8] + arrived[:, 8:]
    small = lax.broadcasted_iota(jnp.int32, (8, 128), 1)
    top = jnp.max(st, axis=0)
    total = jnp.zeros((16, 256), F32)
    den = jnp.zeros((8, 128), F32)
    for i in range(CHIPS):
        f = jnp.where(small < 64, jnp.exp(st[i] - top), 0.0)
        den = den + st[i] * pltpu.roll(f, 64, 1)
        scale = jnp.concatenate([widened(f, 0, 4), widened(f, 4, 4)], 0)
        total = total + land[i, :, :256].astype(F32) * scale
    scale = jnp.concatenate([widened(den, 64, 4), widened(den, 68, 4)], 0)
    attn[...] = (total / scale).astype(BF)

    block = gath.at[rows_of(chip * 16, 16)]
    pltpu.make_async_copy(attn, block, bar4.at[0]).start()

    def attn_start(i, _):
        to = lax.rem(chip + i, CHIPS)
        remote(attn, block, one.at[9], bar4.at[0], to, core, head).start()
        return 0

    lax.fori_loop(1, CHIPS, attn_start, 0)
    video(3, 6)
    remote(gath, gath, one.at[9], bar4.at[0], chip, 1 - core, head).wait_recv()
    swap_w.wait_recv()
    acc = None
    for h in range(2):
        weights = wide[:, h * 256 : (h + 1) * 256]
        r = lax.dot_general(gath[...], weights, NT, preferred_element_type=F32)
        r = r.reshape(CHIPS, 16, 64)[:, h * 8 : (h + 1) * 8]
        acc = r if acc is None else acc + r
    flat = acc.reshape(256, 64).T
    for k in range(2):
        for h in range(2):
            part[k, h] = flat[k * 32 : (k + 1) * 32, h * 128 : (h + 1) * 128]
    across = [
        remote(part.at[1, head], back.at[0], last.at[2], last.at[3], chip, 1 - core, head),
        remote(part.at[0, 1 - head], back.at[1], last.at[4], last.at[5], chip, core, 1 - head),
        remote(part.at[1, 1 - head], back.at[2], last.at[6], last.at[7], chip, 1 - core, 1 - head),
    ]
    for copy in across:
        copy.start()
    video(6, PAIRS)
    total = part[0, head]
    for i, copy in enumerate(across):
        copy.wait_recv()
        total = total + back[i]
    out[...] = total.astype(BF)

    for copy in across:
        copy.wait_send()
    swap_w.wait_send()
    end_first()
    most = gath.at[pl.ds(0, (CHIPS - 1) * 16)]
    remote(most, most, one.at[9], bar4.at[0], chip, 1 - core, head).wait_send()
    remote(others, others, one.at[7], one.at[8], chip, 1 - core, head).wait_send()
    send_n.wait_send()
    send_s.wait_send()
    for j in range(PAIRS):
        pair_copy(j).wait()
    for count, holds in ((15, same_quarter), (16, jnp.logical_not(same_quarter))):

        @pl.when(holds)
        def _(count=count):
            weights = wl.at[pl.ds(0, count)]
            remote(weights, weights, one.at[0], one.at[1], chip, 1 - core, head).wait_send()


def main_part(x, w, vclip, aclip, kv, vq, wout):
    n = vq.shape[0]
    dma = pltpu.SemaphoreType.DMA
    return pl.pallas_call(
        main_kernel,
        out_shape=(
            jax.ShapeDtypeStruct((n, 128 * PAIRS), BF),
            jax.ShapeDtypeStruct((32, 128), BF),
        ),
        in_specs=[HBM] * 7,
        out_specs=(HBM, VMEM),
        scratch_shapes=[
            pltpu.VMEM((128, 768), BF),
            pltpu.VMEM((256, 2048), BF),
            pltpu.VMEM((16, 128), jnp.int32),
            pltpu.VMEM((2, 128), jnp.int32),
            pltpu.VMEM((n, 1024), BF),
            pltpu.VMEM((n, 1024), BF),
            pltpu.VMEM((n, 1024), BF),
            pltpu.VMEM((32, 1024), BF),
            pltpu.VMEM((n, 128 * PAIRS), BF),
            pltpu.VMEM((768, 128), BF),
            pltpu.VMEM((16, 48, 128), BF),
            pltpu.VMEM((48, 256), BF),
            pltpu.VMEM((3072, 256), BF),
            pltpu.VMEM((n, 128), BF),
            pltpu.VMEM((256, 128), BF),
            pltpu.VMEM((128, 256), BF),
            pltpu.VMEM((512, n), F32),
            pltpu.VMEM((512, n), F32),
            pltpu.VMEM((512, 128), F32),
            pltpu.VMEM((512, 128), F32),
            pltpu.VMEM((2, 256, 512), F32),
            pltpu.VMEM((2, 256, 128), F32),
            pltpu.VMEM((256, 512), F32),
            pltpu.VMEM((256, 128), F32),
            pltpu.VMEM((CHIPS, 16, 384), BF),
            pltpu.VMEM((CHIPS, 16, 384), BF),
            pltpu.VMEM((16, 256), BF),
            pltpu.VMEM((64, 512), BF),
            pltpu.VMEM((CHIPS * 16, 256), BF),
            pltpu.VMEM((2, 2, 32, 128), F32),
            pltpu.VMEM((3, 32, 128), F32),
            dma((8,)),
            dma((PAIRS,)),
            dma((12,)),
        ]
        + [dma((FIRST + 1,))] * 3
        + [dma((1,)), dma((8,))],
        compiler_params=pltpu.CompilerParams(
            collective_id=0, has_side_effects=True, vmem_limit_bytes=LIMIT
        ),
    )(x, w, vclip, aclip, kv, vq, wout)


def move_kernel(first, projected, vout, out, held, small, read, write, sem):
    n = first.shape[0] // MOVES
    fetch = pltpu.make_async_copy(projected, small, sem.at[0])
    fetch.start()

    def inward(i):
        rows = pl.ds(i * n, n)
        return pltpu.make_async_copy(first.at[rows], held.at[rows], read.at[i])

    def outward(i):
        rows = pl.ds(i * n, n)
        return pltpu.make_async_copy(held.at[rows], vout.at[rows], write.at[i])

    for i in range(MOVES):
        inward(i).start()
    fetch.wait()
    store = pltpu.make_async_copy(small, out, sem.at[1])
    store.start()
    for i in range(MOVES):
        inward(i).wait()
        outward(i).start()
    for i in range(MOVES):
        outward(i).wait()
    store.wait()


def move_part(first, projected):
    dma = pltpu.SemaphoreType.DMA
    return pl.pallas_call(
        move_kernel,
        out_shape=(
            jax.ShapeDtypeStruct(first.shape, BF),
            jax.ShapeDtypeStruct(projected.shape, BF),
        ),
        in_specs=[HBM, HBM],
        out_specs=(HBM, HBM),
        scratch_shapes=[
            pltpu.VMEM(first.shape, BF),
            pltpu.VMEM(projected.shape, BF),
            dma((MOVES,)),
            dma((MOVES,)),
            dma((2,)),
        ],
        compiler_params=pltpu.CompilerParams(vmem_limit_bytes=LIMIT),
    )(first, projected)


def shards(vq, kv, video_clip, x, w, audio_clip, wout):
    vclip = video_clip.reshape(-1, 128)
    aclip = audio_clip.reshape(-1, 128)
    first, projected = main_part(x, w, vclip, aclip, kv, vq, wout.T)
    video_attn, out = move_part(first, projected)
    return video_attn, out.T


def solution(mesh):
    return jax.shard_map(
        shards,
        mesh=mesh,
        in_specs=(
            P("seq", "head"),
            P(None, "seq", "head"),
            P("seq"),
            P(),
            P("seq", None, "head"),
            P(),
            P("head", "seq"),
        ),
        out_specs=(P("seq", "head"), P("head", "seq")),
        check_vma=False,
    )
```
